32 devices in a mesh: group: 2 (over x), blk: 16 (over z, y, core).
Axes of the slice: x: 2, y: 2, z: 4, core: 2. Of those that a mesh axis runs over, the one named last changes fastest.
Arguments:
- features: bfloat16 [65536, 256], P(('group', 'blk')), parts along dimension 0, may hold values from -6 to 6
- cotangent: bfloat16 [65536, 256], P(('group', 'blk')), parts along dimension 0, may hold values from -6 to 6
- adjacency: bfloat16 [256, 8, 128, 128], P('blk'), may hold values from -0.25 to 0.25
- block_cols: int32 [256, 8], P('blk'), may hold values from 0 to 255, as said below
- block_count: int32 [256], P('blk'), may hold values from 2 to 8, as said below
- cluster_block: int32 [256], P('blk'), may hold values from 0 to 63, as said below
- cluster_slot: int32 [256, 128], P('blk'), may hold values from 0 to 127
- w_message: bfloat16 [256, 256], replicated, may hold values from -0.375 to 0.375
- w_upward: bfloat16 [256, 256], replicated, may hold values from -0.375 to 0.375
- w_self: bfloat16 [256, 256], replicated, may hold values from -0.375 to 0.375
- w_coarse: bfloat16 [256, 256], replicated, may hold values from -0.375 to 0.375
Outputs:
- layer_out: bfloat16 [65536, 256], P(('group', 'blk')), parts along dimension 0
- feature_grad: bfloat16 [65536, 256], P(('group', 'blk')), parts along dimension 0
- message_grad: float32 [512, 256], P('group'), parts along dimension 0
- upward_grad: float32 [512, 256], P('group'), parts along dimension 0
- self_grad: float32 [512, 256], P('group'), parts along dimension 0
- coarse_grad: float32 [512, 256], P('group'), parts along dimension 0
The draws below stay inside these ranges and needn't reach their ends.
There are 2 independent parts, one for each index of `group`. The reference program is written for one: setup_inputs(seed, part) draws one part's arguments, and reference() takes and returns one part's arrays. A program takes and returns all parts, laid end to end along the dimension named above; an argument that names none is the same for every part. Nothing has to cross between parts.
Inputs may be any that keep to these rules, and one draw needn't show every extreme that they name: `block_cols`: slot 0 of row block r names r. Slot 1 of a row block among the first half of those held at index d of blk names a block from d * 16 minus half of 16 to d * 16 less one, and of one in the second half a block from (d + 1) * 16 to (d + 1) * 16 plus half of 16, less one, taken modulo 256. Every slot of a row block held at index d of blk names a block from d * 16 minus half of 16 to (d + 1) * 16 plus half of 16, less one, taken modulo 256. `block_count`: the counts of the 16 row blocks held at one index of blk sum to at most 80, and to exactly 80 at some index in every draw, where some row block has 8. `cluster_block`: A row block held at index d of blk names a coarse block from d * 4 minus half of 4 to (d + 1) * 4 plus half of 4, less one, taken modulo 64.
All inputs are finite; a program needn't handle non-finite values.
Results may differ from the reference program's by a relative error of at most 0.0075.
Values may be sent and summed in bfloat16 or wider, within the bound.
A program may use at most 128 MiB of HBM per device.

```python
import math
import jax
import jax.numpy as jnp
from jax import lax

F = 256
BS = 128
EMAX = 8
RB = 16
B_DEV = 80
CB = 4
NB = 256
NCB = 64
NODES = 32768
N_BLK = 16


def draw_block_cols(key, part):
    key = jax.random.fold_in(key, 11)
    key_far, key_near = jax.random.split(key)
    row_ids = jnp.arange(NB, dtype=jnp.int32)
    owners = row_ids // RB
    local = row_ids % RB
    offsets = jax.random.randint(key_far, (NB, EMAX), 0, 2 * RB, dtype=jnp.int32)
    targets = jnp.remainder(owners[:, None] * RB - RB // 2 + offsets, NB)
    near_off = jax.random.randint(key_near, (NB,), 0, RB // 2, dtype=jnp.int32)
    side = jnp.where(local < RB // 2, owners * RB - RB // 2, owners * RB + RB)
    neighbour = jnp.remainder(side + near_off, NB)
    targets = targets.at[:, 1].set(neighbour)
    targets = targets.at[:, 0].set(row_ids)
    return targets.astype(jnp.int32)


def shuffle(subkey):
    return jax.random.permutation(subkey, RB * (EMAX - 2)).astype(jnp.int32)


def draw_block_count(key, part):
    key = jax.random.fold_in(key, 23)
    key_spread, key_busy, key_order, key_rows = jax.random.split(key, 4)
    spare = B_DEV - 2 * RB
    uniform_draw = jax.random.randint(key_spread, (N_BLK,), 0, spare + 1, dtype=jnp.int32)
    extras = uniform_draw * uniform_draw // max(spare, 1)
    busiest = jax.random.randint(key_busy, (), 0, N_BLK, dtype=jnp.int32)
    is_busy = jnp.arange(N_BLK, dtype=jnp.int32) == busiest
    extras = jnp.where(is_busy, spare, extras)
    orders = jax.vmap(shuffle)(jax.random.split(key_order, N_BLK))
    row_perm = jax.random.permutation(key_rows, RB).astype(jnp.int32)
    whole_rows = (row_perm[:, None] * (EMAX - 2) + jnp.arange(EMAX - 2, dtype=jnp.int32)[None, :]).reshape(RB * (EMAX - 2))
    orders = jnp.where(is_busy[:, None], whole_rows[None, :], orders)
    chosen = (orders < extras[:, None]).astype(jnp.int32).reshape(N_BLK, RB, EMAX - 2)
    return (2 + jnp.sum(chosen, axis=2)).reshape(NB).astype(jnp.int32)


def draw_cluster_block(key, part):
    key = jax.random.fold_in(key, 37)
    owners = jnp.arange(NB, dtype=jnp.int32) // RB
    offsets = jax.random.randint(key, (NB,), 0, 2 * CB, dtype=jnp.int32)
    return jnp.remainder(owners * CB - CB // 2 + offsets, NCB).astype(jnp.int32)


def with_ends(array, own_key, least, top_value):
    longest = array.shape.index(max(array.shape))
    spots = []
    for shift in (0, 1):
        where = [jax.random.randint(jax.random.fold_in(own_key, axis), (), 0, length) for axis, length in enumerate(array.shape)]
        where[longest] = (where[longest] + shift) % array.shape[longest]
        spots.append(tuple(where))
    return array.at[spots[0]].set(least).at[spots[1]].set(top_value)


def block_levels(stream_key, shape, cuts, smallest, high):
    def one(dim, shards_of):
        heights = jax.random.uniform(jax.random.fold_in(jax.random.fold_in(stream_key, 6), dim), (shards_of,), jnp.float32, smallest / len(cuts), high / len(cuts))
        return jnp.repeat(jnp.exp(heights), shape[dim] // shards_of).reshape((-1,) + (1,) * (len(shape) - dim - 1))

    level = one(*cuts[0])
    for cut in cuts[1:]:
        level = level * one(*cut)
    return level


def normal_values(stream_key, extent, deviation, most, cuts=(), kind=jnp.bfloat16):
    result = jax.random.normal(stream_key, extent, jnp.float32) * deviation
    if len(cuts) > 0:
        result = block_levels(stream_key, extent, cuts, -0.22, 0.18) * result
    return jnp.clip(result, min=-most, max=most).astype(kind)


def setup_inputs(seed: int = 0, part: int = 0) -> dict:
    key_list = jax.random.split(jax.random.key(seed), 12)
    part_splits = jax.random.split(jax.random.fold_in(key_list[11], part), 12)
    features = normal_values(part_splits[0], (NODES, F), 1.0, 6.0, ((0, 16),))
    cotangent = normal_values(part_splits[1], (NODES, F), 1.0, 6.0, ((0, 16),))
    adjacency = normal_values(key_list[2], (NB, EMAX, BS, BS), (BS * EMAX // 2) ** -0.5, 0.25, ((0, 16),))
    block_cols = draw_block_cols(jax.random.fold_in(key_list[11], 71), part)
    block_count = draw_block_count(jax.random.fold_in(key_list[11], 71), part)
    cluster_block = draw_cluster_block(jax.random.fold_in(key_list[11], 71), part)
    cluster_slot = with_ends(jax.random.randint(key_list[6], (NB, BS), 0, BS), jax.random.fold_in(key_list[6], 1), 0, BS - 1).astype(jnp.int32)
    w_message = normal_values(key_list[7], (F, F), F ** -0.5, 0.375)
    w_upward = normal_values(key_list[8], (F, F), F ** -0.5, 0.375)
    w_self = normal_values(key_list[9], (F, F), F ** -0.5, 0.375)
    w_coarse = normal_values(key_list[10], (F, F), F ** -0.5, 0.375)
    return dict(features=features, cotangent=cotangent, adjacency=adjacency, block_cols=block_cols, block_count=block_count, cluster_block=cluster_block, cluster_slot=cluster_slot, w_message=w_message, w_upward=w_upward, w_self=w_self, w_coarse=w_coarse)


def silu_slope(value, sigma):
    return sigma * (1.0 + value * (1.0 - sigma))

def reference(features, cotangent, adjacency, block_cols, block_count, cluster_block, cluster_slot, w_message, w_upward, w_self, w_coarse):
    highest = lax.Precision.HIGHEST
    feat_blocks = features.reshape(NB, BS, F)
    active = (jnp.arange(EMAX, dtype=jnp.int32)[None, :] < block_count[:, None]).astype(jnp.float32)
    vals_dev = adjacency.reshape(N_BLK, RB, EMAX, BS, BS)
    cols_dev = block_cols.reshape(N_BLK, RB, EMAX).astype(jnp.int32)
    active_dev = active.reshape(N_BLK, RB, EMAX)

    def forward_piece(pieces):
        values, targets, masks = pieces
        picked = feat_blocks[targets].astype(jnp.float32)
        return jnp.einsum('reij,rejf,re->rif', values.astype(jnp.float32), picked, masks, precision=highest)
    aggregate = lax.map(forward_piece, (vals_dev, cols_dev, active_dev)).reshape(NODES, F)
    message = aggregate.astype(jnp.bfloat16)
    slot_onehot = (cluster_slot[:, :, None] == jnp.arange(BS, dtype=jnp.int32)[None, None, :]).astype(jnp.float32)
    partial_pool = jnp.einsum('rij,rif->rjf', slot_onehot, feat_blocks.astype(jnp.float32), precision=highest)
    pooled_sum = jnp.zeros((NCB, BS, F), jnp.float32).at[cluster_block].add(partial_pool)
    pooled = (0.25 * pooled_sum).astype(jnp.bfloat16).reshape(NCB * BS, F)
    coarse_pre = jnp.dot(pooled, w_coarse, preferred_element_type=jnp.float32)
    coarse_sig = jax.nn.sigmoid(coarse_pre)
    coarse = (coarse_pre * coarse_sig).astype(jnp.bfloat16).reshape(NCB, BS, F)
    upward = coarse[cluster_block[:, None], cluster_slot].reshape(NODES, F)
    pre_act = jnp.dot(message, w_message, preferred_element_type=jnp.float32)
    pre_act = pre_act + jnp.dot(upward, w_upward, preferred_element_type=jnp.float32)
    pre_act = pre_act + jnp.dot(features, w_self, preferred_element_type=jnp.float32)
    sigma = jax.nn.sigmoid(pre_act)
    layer_out = (features.astype(jnp.float32) + pre_act * sigma).astype(jnp.bfloat16)
    grad_pre = (cotangent.astype(jnp.float32) * silu_slope(pre_act, sigma)).astype(jnp.bfloat16)
    scale = 1.0 / math.sqrt(NODES)
    message_grad = jnp.dot(message.T, grad_pre, preferred_element_type=jnp.float32) * scale
    upward_grad = jnp.dot(upward.T, grad_pre, preferred_element_type=jnp.float32) * scale
    self_grad = jnp.dot(features.T, grad_pre, preferred_element_type=jnp.float32) * scale
    back_message = jnp.dot(grad_pre, w_message.T, preferred_element_type=jnp.float32).astype(jnp.bfloat16)
    back_upward = jnp.dot(grad_pre, w_upward.T, preferred_element_type=jnp.float32).astype(jnp.bfloat16)
    back_self = jnp.dot(grad_pre, w_self.T, preferred_element_type=jnp.float32)
    back_dev = back_message.reshape(N_BLK, RB, BS, F)

    def backward_step(carry, pieces):
        values, targets, masks, grads = pieces
        contrib = jnp.einsum('reij,rif,re->rejf', values.astype(jnp.float32), grads.astype(jnp.float32), masks, precision=highest)
        carry = carry.at[targets.reshape(RB * EMAX)].add(contrib.reshape(RB * EMAX, BS, F))
        return (carry, None)
    back_aggregate, unused = lax.scan(backward_step, jnp.zeros((NB, BS, F), jnp.float32), (vals_dev, cols_dev, active_dev, back_dev))
    coarse_part = jnp.einsum('rij,rif->rjf', slot_onehot, back_upward.reshape(NB, BS, F).astype(jnp.float32), precision=highest)
    coarse_back = jnp.zeros((NCB, BS, F), jnp.float32).at[cluster_block].add(coarse_part)
    grad_coarse_pre = (coarse_back.reshape(NCB * BS, F) * silu_slope(coarse_pre, coarse_sig)).astype(jnp.bfloat16)
    coarse_grad = jnp.dot(pooled.T, grad_coarse_pre, preferred_element_type=jnp.float32) * scale
    back_pooled = jnp.dot(grad_coarse_pre, w_coarse.T, preferred_element_type=jnp.float32).astype(jnp.bfloat16).reshape(NCB, BS, F)
    spread = back_pooled[cluster_block[:, None], cluster_slot].reshape(NODES, F).astype(jnp.float32)
    total = cotangent.astype(jnp.float32) + back_aggregate.reshape(NODES, F) + back_self + 0.25 * spread
    feature_grad = total.astype(jnp.bfloat16)
    return (layer_out, feature_grad, message_grad, upward_grad, self_grad, coarse_grad)
```

```python
import functools
import math

import jax
import jax.numpy as jnp
from jax import lax
from jax.experimental import pallas as pl
from jax.experimental.pallas import tpu as pltpu
from jax.sharding import PartitionSpec as P

MESH = pl.DeviceIdType.MESH
BF16 = jnp.bfloat16
F32 = jnp.float32


def mm(left, right):
    return lax.dot_general(left, right, (((1,), (0,)), ((), ())), preferred_element_type=F32)


def mm_nt(left, right):
    return lax.dot_general(left, right, (((1,), (1,)), ((), ())), preferred_element_type=F32)


def mm_tn(left, right):
    return lax.dot_general(left, right, (((0,), (0,)), ((), ())), preferred_element_type=F32)


def slope(value, sigma):
    return sigma * (1.0 + value * (1.0 - sigma))


def stages_of(count):
    stages, stride, rest = [], 1, count
    if rest % 2 == 0:
        stages.append((stride, 2))
        stride, rest = stride * 2, rest // 2
    while rest > 1:
        bits = rest.bit_length() - 1
        radix = 4 if rest % 4 == 0 and bits % 2 == 0 else 2
        stages.append((stride, radix))
        stride, rest = stride * radix, rest // radix
    return stages


def kernel(
    dims,
    meta,
    slot,
    w_m,
    w_u,
    w_s,
    w_c,
    feats,
    cots,
    adjs,
    layer_out,
    feature_grad,
    grad_m,
    grad_u,
    grad_s,
    grad_c,
    near,
    adj,
    adj_t,
    cot,
    total,
    msg,
    up,
    grad,
    back_m,
    hot_t,
    hot,
    chain,
    pool_chain,
    pool_send,
    pool_recv,
    pooled,
    coarse,
    c_slope,
    back_send,
    back_recv,
    back_pooled,
    row_send,
    row_recv,
    out_buf,
    acc,
    ring_send,
    ring_recv,
    gathered,
    local_sem,
    out_sem,
    ex_send,
    ex_recv,
    rs_send,
    rs_recv,
    ag_send,
    ag_recv,
):
    n, rb, slots, bs, cb = dims
    width = near.shape[2]
    half, edge, win = rb // 2, cb // 2, 2 * cb
    me = lax.axis_index("blk")
    left, right = lax.rem(me + n - 1, n), lax.rem(me + 1, n)
    stages = stages_of(n)
    o_prev = rb * slots
    o_last = 2 * rb * slots
    o_cidx = o_last + 2 * rb
    o_prevc = o_cidx + rb
    o_lastc = o_prevc + rb

    get_feats = pltpu.make_async_copy(feats, near.at[pl.ds(half, rb)], local_sem.at[0])
    get_cot = pltpu.make_async_copy(cots, cot, local_sem.at[1])
    get_adj = pltpu.make_async_copy(adjs, adj, local_sem.at[2])
    get_feats.start()
    get_adj.start()
    get_cot.start()

    barrier = pltpu.get_barrier_semaphore()
    friends = [left, right]
    for stride, radix in stages:
        digit = lax.rem(me // stride, radix)
        for off in range(1, radix):
            friends.append(me + (lax.rem(digit + off, radix) - digit) * stride)
    for friend in friends:
        pl.semaphore_signal(barrier, inc=1, device_id={"blk": friend}, device_id_type=MESH)
    near[2 * rb] = jnp.zeros((bs, width), BF16)
    pool_chain[rb] = jnp.zeros((bs, width), F32)
    chain[rb * slots] = jnp.zeros((bs, width), F32)
    get_feats.wait()
    pl.semaphore_wait(barrier, len(friends))

    def remote(src, dst, index, to):
        return pltpu.make_async_remote_copy(
            src_ref=src,
            dst_ref=dst,
            send_sem=ex_send.at[index],
            recv_sem=ex_recv.at[index],
            device_id={"blk": to},
            device_id_type=MESH,
        )

    halo = [
        remote(near.at[pl.ds(half, half)], near.at[pl.ds(rb + half, half)], 0, left),
        remote(near.at[pl.ds(rb, half)], near.at[pl.ds(0, half)], 1, right),
    ]
    for copy in halo:
        copy.start()

    def pool_body(r, carry):
        row = slot[pl.ds(r, 1), :]
        ids = lax.broadcasted_iota(jnp.int32, (bs, bs), 0)
        one = jnp.where(ids == row, 1.0, 0.0).astype(BF16)
        hot_t[r] = one
        pool_chain[r] = mm(one, near[half + r]) + pool_chain[meta[o_prevc + r]]
        return carry

    lax.fori_loop(0, rb, pool_body, 0, unroll=2)
    for w in range(win):
        pool_send[w] = pool_chain[meta[o_lastc + w]].astype(BF16)
    pool_ex = [
        remote(pool_send.at[pl.ds(0, cb)], pool_recv.at[pl.ds(cb, cb)], 2, left),
        remote(pool_send.at[pl.ds(cb, cb)], pool_recv.at[pl.ds(0, cb)], 3, right),
    ]
    for copy in pool_ex:
        copy.start()

    quad = 4

    def self_body(q, carry):
        x = near[pl.ds(half + q * quad, quad)].reshape(quad * bs, width)
        total[pl.ds(q * quad, quad)] = mm(x, w_s[...]).reshape(quad, bs, width)
        for k in range(quad):
            hot[q * quad + k] = hot_t[q * quad + k].T
        return carry

    lax.fori_loop(0, rb // quad, self_body, 0)
    get_adj.wait()

    def flip_body(r, carry):
        for e in range(slots):
            adj_t[r, pl.ds(e * bs, bs), :] = adj[r, e].T
        return carry

    lax.fori_loop(0, rb, flip_body, 0)

    for copy in pool_ex:
        copy.wait()
    for w in range(win):
        summed = pool_chain[meta[o_lastc + w]] + pool_recv[w].astype(F32)
        pooled[pl.ds(w * bs, bs), :] = (0.25 * summed).astype(BF16)
    pre = mm(pooled[...], w_c[...])
    sig = jax.nn.sigmoid(pre)
    coarse[...] = (pre * sig).astype(BF16).reshape(win, bs, width)
    c_slope[...] = slope(pre, sig)

    def up_body(q, carry):
        parts = []
        for k in range(quad):
            r = q * quad + k
            parts.append(mm(hot[r], coarse[meta[o_cidx + r]]).astype(BF16))
        block = jnp.concatenate(parts, axis=0)
        up[pl.ds(q * quad, quad)] = block.reshape(quad, bs, width)
        total[pl.ds(q * quad, quad)] += mm(block, w_u[...]).reshape(quad, bs, width)
        return carry

    lax.fori_loop(0, rb // quad, up_body, 0)
    get_cot.wait()
    for copy in halo:
        copy.wait()

    def fine_body(q, carry):
        parts = []
        for k in range(quad):
            r = q * quad + k
            lhs = jnp.concatenate([adj[r, e] for e in range(slots)], axis=1)
            rhs = jnp.concatenate([near[meta[r * slots + e]] for e in range(slots)], axis=0)
            parts.append(mm(lhs, rhs).astype(BF16))
        rows = pl.ds(q * quad, quad)
        flat = (quad * bs, width)
        message = jnp.concatenate(parts, axis=0)
        msg[rows] = message.reshape(quad, bs, width)
        pre = total[rows].reshape(flat) + mm(message, w_m[...])
        sig = jax.nn.sigmoid(pre)
        x = near[pl.ds(half + q * quad, quad)].reshape(flat).astype(F32)
        out_buf[rows] = (x + pre * sig).astype(BF16).reshape(quad, bs, width)
        c = cot[rows].reshape(flat).astype(F32)
        g = (c * slope(pre, sig)).astype(BF16)
        grad[rows] = g.reshape(quad, bs, width)
        back_m[rows] = mm_nt(g, w_m[...]).astype(BF16).reshape(quad, bs, width)
        total[rows] = (c + mm_nt(g, w_s[...])).reshape(quad, bs, width)
        back_u = mm_nt(g, w_u[...]).astype(BF16)
        for k in range(quad):
            r = q * quad + k
            part = mm(hot_t[r], back_u[k * bs : (k + 1) * bs])
            pool_chain[r] = part + pool_chain[meta[o_prevc + r]]
        return carry

    lax.fori_loop(0, rb // quad, fine_body, 0)
    put_out = pltpu.make_async_copy(out_buf, layer_out, out_sem.at[0])
    put_out.start()
    for w in range(win):
        back_send[w] = pool_chain[meta[o_lastc + w]].astype(BF16)
    back_ex = [
        remote(back_send.at[pl.ds(0, cb)], back_recv.at[pl.ds(cb, cb)], 4, left),
        remote(back_send.at[pl.ds(cb, cb)], back_recv.at[pl.ds(0, cb)], 5, right),
    ]
    for copy in back_ex:
        copy.start()

    scale = 1.0 / math.sqrt(n * rb * bs)
    acc[...] = jnp.zeros_like(acc)

    def grads_body(q, carry):
        rows = pl.ds(q * quad, quad)
        flat = (quad * bs, width)
        g = grad[rows].reshape(flat)
        x = near[pl.ds(half + q * quad, quad)].reshape(flat)
        acc[pl.ds(0, width)] += mm_tn(msg[rows].reshape(flat), g)
        acc[pl.ds(width, width)] += mm_tn(up[rows].reshape(flat), g)
        acc[pl.ds(2 * width, width)] += mm_tn(x, g)
        return carry

    lax.fori_loop(0, rb // quad, grads_body, 0)

    def coarse_body(w, carry):
        rows = pl.ds(pl.multiple_of(w * bs, bs), bs)
        part = (pool_chain[meta[o_lastc + w]] * c_slope[rows, :]).astype(BF16)
        acc[pl.ds(3 * width, width)] += mm_tn(pooled[rows, :], part)
        return carry

    lax.fori_loop(0, win, coarse_body, 0)
    acc[...] = acc[...] * scale

    height = acc.shape[0]
    plan = []
    base, seg, index, slot_row = 0, height, 0, 0
    for stride, radix in stages:
        digit = lax.rem(me // stride, radix)
        sub = seg // radix
        plan.append((stride, radix, digit, base, seg, sub, index, slot_row))
        base = base + digit * sub
        seg = sub
        slot_row += (radix - 1) * sub
        index += radix - 1

    def rows_at(start, count):
        return pl.ds(pl.multiple_of(start, 16), count)

    def scatter_start(k):
        stride, radix, digit, base, seg, sub, index, slot_row = plan[k]
        ring_send[k, rows_at(base, seg), :] = acc[rows_at(base, seg), :].astype(BF16)
        copies = []
        for off in range(1, radix):
            other = lax.rem(digit + off, radix)
            copies.append(
                pltpu.make_async_remote_copy(
                    src_ref=ring_send.at[k, rows_at(base + other * sub, sub), :],
                    dst_ref=ring_recv.at[pl.ds(slot_row + (off - 1) * sub, sub), :],
                    send_sem=rs_send.at[index + off - 1],
                    recv_sem=rs_recv.at[index + off - 1],
                    device_id={"blk": me + (other - digit) * stride},
                    device_id_type=MESH,
                )
            )
        for copy in copies:
            copy.start()
        return copies

    def scatter_end(k, copies):
        stride, radix, digit, base, seg, sub, index, slot_row = plan[k]
        for copy in copies:
            copy.wait()
        mine = rows_at(base + digit * sub, sub)
        value = acc[mine, :]
        for off in range(1, radix):
            value = value + ring_recv[pl.ds(slot_row + (off - 1) * sub, sub), :].astype(F32)
        acc[mine, :] = value

    def gather_start(k):
        stride, radix, digit, base, seg, sub, index, slot_row = plan[k]
        mine = rows_at(base + digit * sub, sub)
        copies = []
        for off in range(1, radix):
            other = lax.rem(digit + off, radix)
            copies.append(
                pltpu.make_async_remote_copy(
                    src_ref=gathered.at[mine, :],
                    dst_ref=gathered.at[mine, :],
                    send_sem=ag_send.at[index + off - 1],
                    recv_sem=ag_recv.at[index + off - 1],
                    device_id={"blk": me + (other - digit) * stride},
                    device_id_type=MESH,
                )
            )
        for copy in copies:
            copy.start()
        return copies

    flying = scatter_start(0)

    def flow_body(r, carry):
        prod = mm(adj_t[r], back_m[r])
        for e in range(slots):
            s = r * slots + e
            chain[s] = prod[e * bs : (e + 1) * bs] + chain[meta[o_prev + s]]
        return carry

    lax.fori_loop(0, rb, flow_body, 0)
    for b in range(half):
        row_send[b] = chain[meta[o_last + b]].astype(BF16)
        row_send[half + b] = chain[meta[o_last + half + rb + b]].astype(BF16)
    row_ex = [
        remote(row_send.at[pl.ds(0, half)], row_recv.at[pl.ds(half, half)], 6, left),
        remote(row_send.at[pl.ds(half, half)], row_recv.at[pl.ds(0, half)], 7, right),
    ]
    for copy in row_ex:
        copy.start()

    scatter_end(0, flying)
    if len(stages) > 1:
        flying = scatter_start(1)

    for copy in back_ex:
        copy.wait()
    for w in range(win):
        rows = pl.ds(w * bs, bs)
        summed = pool_chain[meta[o_lastc + w]] + back_recv[w].astype(F32)
        g = (summed * c_slope[rows, :]).astype(BF16)
        back_pooled[w] = mm_nt(g, w_c[...]).astype(BF16)

    def spread_body(r, carry):
        spread = mm(hot[r], back_pooled[meta[o_cidx + r]])
        total[r] += 0.25 * spread + chain[meta[o_last + half + r]]
        return carry

    lax.fori_loop(0, rb, spread_body, 0, unroll=2)

    done = 1
    if len(stages) > 1:
        scatter_end(1, flying)
        done = 2
    if len(stages) > 2:
        flying = scatter_start(2)

    put_out.wait()
    for copy in row_ex:
        copy.wait()

    def last_body(r, carry):
        out_buf[r] = (total[r] + row_recv[r].astype(F32)).astype(BF16)
        return carry

    lax.fori_loop(0, rb, last_body, 0, unroll=2)
    put_grad = pltpu.make_async_copy(out_buf, feature_grad, out_sem.at[1])
    put_grad.start()

    if len(stages) > 2:
        scatter_end(2, flying)
        done = 3
    for k in range(done, len(stages)):
        scatter_end(k, scatter_start(k))
    stride, radix, digit, base, seg, sub, index, slot_row = plan[-1]
    mine = rows_at(base + digit * sub, sub)
    gathered[mine, :] = acc[mine, :].astype(BF16)
    for k in reversed(range(len(stages))):
        for copy in gather_start(k):
            copy.wait()
    for k, out in enumerate((grad_m, grad_u, grad_s, grad_c)):
        out[...] = gathered[pl.ds(k * width, width), :].astype(F32)
    put_grad.wait()


def on_device(
    features,
    cotangent,
    adjacency,
    block_cols,
    block_count,
    cluster_block,
    cluster_slot,
    w_message,
    w_upward,
    w_self,
    w_coarse,
):
    rb, slots = block_cols.shape
    bs = adjacency.shape[2]
    width = features.shape[1]
    n = lax.axis_size("blk")
    position = lax.axis_index("blk")
    cb = rb // 4
    half, edge, win = rb // 2, cb // 2, 2 * cb
    count = rb * slots

    live = jnp.arange(slots, dtype=jnp.int32)[None, :] < block_count[:, None]
    cols = jnp.clip(jnp.remainder(block_cols - (position * rb - half), n * rb), 0, 2 * rb - 1)
    cols = jnp.where(live, cols, 2 * rb).reshape(count)
    alive = live.reshape(count)
    ids = jnp.arange(count, dtype=jnp.int32)
    same = (cols[:, None] == cols[None, :]) & alive[None, :] & (ids[None, :] < ids[:, None])
    prev = jnp.max(jnp.where(same, ids[None, :], -1), axis=1)
    prev = jnp.where(prev < 0, count, prev)
    wins = jnp.arange(2 * rb, dtype=jnp.int32)
    last = jnp.max(jnp.where(cols[None, :] == wins[:, None], ids[None, :], -1), axis=1)
    last = jnp.where(last < 0, count, last)
    cidx = jnp.clip(jnp.remainder(cluster_block - (position * cb - edge), n * cb), 0, win - 1)
    rids = jnp.arange(rb, dtype=jnp.int32)
    samec = (cidx[:, None] == cidx[None, :]) & (rids[None, :] < rids[:, None])
    prevc = jnp.max(jnp.where(samec, rids[None, :], -1), axis=1)
    prevc = jnp.where(prevc < 0, rb, prevc)
    cwins = jnp.arange(win, dtype=jnp.int32)
    lastc = jnp.max(jnp.where(cidx[None, :] == cwins[:, None], rids[None, :], -1), axis=1)
    lastc = jnp.where(lastc < 0, rb, lastc)
    meta = jnp.concatenate([cols, prev, last, cidx, prevc, lastc])

    stages = stages_of(n)
    links = max(sum(radix - 1 for _, radix in stages), 1)
    height = 4 * width
    rows, seg = 0, height
    for _, radix in stages:
        seg //= radix
        rows += (radix - 1) * seg
    vmem = pl.BlockSpec(memory_space=pltpu.VMEM)
    hbm = pl.BlockSpec(memory_space=pl.ANY)
    blocks = (rb, bs, width)
    outs = pl.pallas_call(
        functools.partial(kernel, (n, rb, slots, bs, cb)),
        out_shape=[
            jax.ShapeDtypeStruct(blocks, BF16),
            jax.ShapeDtypeStruct(blocks, BF16),
        ]
        + [jax.ShapeDtypeStruct((width, width), F32)] * 4,
        in_specs=[pl.BlockSpec(memory_space=pltpu.SMEM)] + [vmem] * 5 + [hbm] * 3,
        out_specs=[hbm, hbm] + [vmem] * 4,
        scratch_shapes=[
            pltpu.VMEM((2 * rb + 1, bs, width), BF16),
            pltpu.VMEM((rb, slots, bs, bs), BF16),
            pltpu.VMEM((rb, slots * bs, bs), BF16),
            pltpu.VMEM(blocks, BF16),
            pltpu.VMEM(blocks, F32),
            pltpu.VMEM(blocks, BF16),
            pltpu.VMEM(blocks, BF16),
            pltpu.VMEM(blocks, BF16),
            pltpu.VMEM(blocks, BF16),
            pltpu.VMEM((rb, bs, bs), BF16),
            pltpu.VMEM((rb, bs, bs), BF16),
            pltpu.VMEM((count + 1, bs, width), F32),
            pltpu.VMEM((rb + 1, bs, width), F32),
            pltpu.VMEM((win, bs, width), BF16),
            pltpu.VMEM((win, bs, width), BF16),
            pltpu.VMEM((win * bs, width), BF16),
            pltpu.VMEM((win, bs, width), BF16),
            pltpu.VMEM((win * bs, width), F32),
            pltpu.VMEM((win, bs, width), BF16),
            pltpu.VMEM((win, bs, width), BF16),
            pltpu.VMEM((win, bs, width), BF16),
            pltpu.VMEM(blocks, BF16),
            pltpu.VMEM(blocks, BF16),
            pltpu.VMEM(blocks, BF16),
            pltpu.VMEM((height, width), F32),
            pltpu.VMEM((max(len(stages), 1), height, width), BF16),
            pltpu.VMEM((max(rows, 16), width), BF16),
            pltpu.VMEM((height, width), BF16),
            pltpu.SemaphoreType.DMA((3,)),
            pltpu.SemaphoreType.DMA((2,)),
            pltpu.SemaphoreType.DMA((8,)),
            pltpu.SemaphoreType.DMA((8,)),
            pltpu.SemaphoreType.DMA((links,)),
            pltpu.SemaphoreType.DMA((links,)),
            pltpu.SemaphoreType.DMA((links,)),
            pltpu.SemaphoreType.DMA((links,)),
        ],
        compiler_params=pltpu.CompilerParams(
            collective_id=0, has_side_effects=True, vmem_limit_bytes=56 * 1024 * 1024
        ),
    )(
        meta,
        cluster_slot,
        w_message,
        w_upward,
        w_self,
        w_coarse,
        features.reshape(blocks),
        cotangent.reshape(blocks),
        adjacency,
    )
    return (outs[0].reshape(features.shape), outs[1].reshape(features.shape), *outs[2:])


def solution(mesh):
    in_specs = (
        P(("group", "blk"), None),
        P(("group", "blk"), None),
        P("blk", None, None, None),
        P("blk", None),
        P("blk"),
        P("blk"),
        P("blk", None),
        P(),
        P(),
        P(),
        P(),
    )
    out_specs = (
        P(("group", "blk"), None),
        P(("group", "blk"), None),
        P("group", None),
        P("group", None),
        P("group", None),
        P("group", None),
    )
    return jax.shard_map(
        on_device, mesh=mesh, in_specs=in_specs, out_specs=out_specs, check_vma=False
    )
```

```python
import functools
import math

import jax
import jax.numpy as jnp
from jax import lax
from jax.experimental import pallas as pl
from jax.experimental.pallas import tpu as pltpu
from jax.sharding import PartitionSpec as P

MESH = pl.DeviceIdType.MESH
BF16 = jnp.bfloat16
F32 = jnp.float32


def mm(left, right):
    return lax.dot_general(left, right, (((1,), (0,)), ((), ())), preferred_element_type=F32)


def mm_nt(left, right):
    return lax.dot_general(left, right, (((1,), (1,)), ((), ())), preferred_element_type=F32)


def mm_tn(left, right):
    return lax.dot_general(left, right, (((0,), (0,)), ((), ())), preferred_element_type=F32)


def slope(value, sigma):
    return sigma * (1.0 + value * (1.0 - sigma))


def stages_of(count):
    stages, stride, rest = [], 1, count
    if rest % 2 == 0:
        stages.append((stride, 2))
        stride, rest = stride * 2, rest // 2
    while rest > 1:
        bits = rest.bit_length() - 1
        radix = 4 if rest % 4 == 0 and bits % 2 == 0 else 2
        stages.append((stride, radix))
        stride, rest = stride * radix, rest // radix
    return stages[:1] + stages[1:][::-1]


def order_kernel(dims, cols_in, counts, clusters, meta):
    n, rb, slots, cb = dims
    half, edge, win = rb // 2, cb // 2, 2 * cb
    me = lax.axis_index("blk")
    count = rb * slots
    o_prev = count
    o_last = 2 * count
    o_cidx = o_last + 2 * rb
    o_prevc = o_cidx + rb
    o_lastc = o_prevc + rb

    def fill(start, size, value):
        def body(i, carry):
            meta[start + i] = value
            return carry

        lax.fori_loop(0, size, body, 0, unroll=8)

    fill(o_last, 2 * rb, count)
    fill(o_lastc, win, rb)

    def row(r, carry):
        live = counts[r]
        for e in range(slots):
            s = r * slots + e
            there = cols_in[r, e] - (me * rb - half)
            there = jnp.where(there < 0, there + n * rb, there)
            there = jnp.where(there >= n * rb, there - n * rb, there)
            there = jnp.minimum(jnp.maximum(there, 0), 2 * rb - 1)
            on = e < live
            before = meta[o_last + there]
            meta[s] = jnp.where(on, there, 2 * rb)
            meta[o_prev + s] = jnp.where(on, before, count)
            meta[o_last + there] = jnp.where(on, s, before)
        c = clusters[r] - (me * cb - edge)
        c = jnp.where(c < 0, c + n * cb, c)
        c = jnp.where(c >= n * cb, c - n * cb, c)
        c = jnp.minimum(jnp.maximum(c, 0), win - 1)
        meta[o_cidx + r] = c
        meta[o_prevc + r] = meta[o_lastc + c]
        meta[o_lastc + c] = r
        return carry

    lax.fori_loop(0, rb, row, 0)


def finish_kernel(pieces, a, b, g, a_out, b_out, m_out, u_out, s_out, c_out, buf, sem):
    copies = []
    step = a.shape[0] // pieces
    for k in range(pieces):
        rows = pl.ds(k * step, step)
        copies.append(pltpu.make_async_copy(a.at[rows], a_out.at[rows], sem.at[2 * k]))
        copies.append(pltpu.make_async_copy(b.at[rows], b_out.at[rows], sem.at[2 * k + 1]))
    load = pltpu.make_async_copy(g, buf, sem.at[2 * pieces])
    load.start()
    for copy in copies:
        copy.start()
    load.wait()
    width = m_out.shape[0]
    for k, out in enumerate((m_out, u_out, s_out, c_out)):
        out[...] = buf[pl.ds(k * width, width), :].astype(F32)
    for copy in copies:
        copy.wait()


def kernel(
    dims,
    meta,
    slot,
    w_m,
    w_u,
    w_s,
    w_c,
    feats,
    cots,
    adjs,
    layer_out,
    feature_grad,
    gathered,
    near,
    adj,
    adj_t,
    cot,
    total,
    msg,
    up,
    grad,
    back_m,
    hot_t,
    hot,
    chain,
    pool_chain,
    pool_send,
    pool_recv,
    pooled,
    coarse,
    c_slope,
    back_send,
    back_recv,
    back_pooled,
    row_send,
    row_recv,
    out_buf,
    acc,
    ring_send,
    ring_recv,
    local_sem,
    out_sem,
    ex_send,
    ex_recv,
    rs_send,
    rs_recv,
    ag_send,
    ag_recv,
):
    n, rb, slots, bs, cb = dims
    width = near.shape[2]
    half, edge, win = rb // 2, cb // 2, 2 * cb
    me = lax.axis_index("blk")
    left, right = lax.rem(me + n - 1, n), lax.rem(me + 1, n)
    stages = stages_of(n)
    o_prev = rb * slots
    o_last = 2 * rb * slots
    o_cidx = o_last + 2 * rb
    o_prevc = o_cidx + rb
    o_lastc = o_prevc + rb

    get_feats = pltpu.make_async_copy(feats, near.at[pl.ds(half, rb)], local_sem.at[0])
    get_cot = pltpu.make_async_copy(cots, cot, local_sem.at[1])
    get_adj = pltpu.make_async_copy(adjs, adj, local_sem.at[2])
    get_feats.start()
    get_adj.start()
    get_cot.start()

    barrier = pltpu.get_barrier_semaphore()
    friends = [left, right]
    for stride, radix in stages:
        digit = lax.rem(me // stride, radix)
        for off in range(1, radix):
            friends.append(me + (lax.rem(digit + off, radix) - digit) * stride)
    for friend in friends:
        pl.semaphore_signal(barrier, inc=1, device_id={"blk": friend}, device_id_type=MESH)
    near[2 * rb] = jnp.zeros((bs, width), BF16)
    pool_chain[rb] = jnp.zeros((bs, width), F32)
    chain[rb * slots] = jnp.zeros((bs, width), F32)
    get_feats.wait()
    pl.semaphore_wait(barrier, len(friends))

    def remote(src, dst, index, to):
        return pltpu.make_async_remote_copy(
            src_ref=src,
            dst_ref=dst,
            send_sem=ex_send.at[index],
            recv_sem=ex_recv.at[index],
            device_id={"blk": to},
            device_id_type=MESH,
        )

    halo = [
        remote(near.at[pl.ds(half, half)], near.at[pl.ds(rb + half, half)], 0, left),
        remote(near.at[pl.ds(rb, half)], near.at[pl.ds(0, half)], 1, right),
    ]
    for copy in halo:
        copy.start()

    def pool_body(r, carry):
        row = slot[pl.ds(r, 1), :]
        ids = lax.broadcasted_iota(jnp.int32, (bs, bs), 0)
        one = jnp.where(ids == row, 1.0, 0.0).astype(BF16)
        hot_t[r] = one
        pool_chain[r] = mm(one, near[half + r]) + pool_chain[meta[o_prevc + r]]
        return carry

    lax.fori_loop(0, rb, pool_body, 0, unroll=2)
    for w in range(win):
        pool_send[w] = pool_chain[meta[o_lastc + w]].astype(BF16)
    pool_ex = [
        remote(pool_send.at[pl.ds(0, cb)], pool_recv.at[pl.ds(cb, cb)], 2, left),
        remote(pool_send.at[pl.ds(cb, cb)], pool_recv.at[pl.ds(0, cb)], 3, right),
    ]
    for copy in pool_ex:
        copy.start()

    quad = 4

    def self_body(q, carry):
        x = near[pl.ds(half + q * quad, quad)].reshape(quad * bs, width)
        total[pl.ds(q * quad, quad)] = mm(x, w_s[...]).reshape(quad, bs, width)
        for k in range(quad):
            hot[q * quad + k] = hot_t[q * quad + k].T
        return carry

    lax.fori_loop(0, rb // quad, self_body, 0)
    get_adj.wait()

    def flip_body(r, carry):
        for e in range(slots):
            adj_t[r, pl.ds(e * bs, bs), :] = adj[r, e].T
        return carry

    lax.fori_loop(0, rb, flip_body, 0)

    for copy in pool_ex:
        copy.wait()
    for w in range(win):
        summed = pool_chain[meta[o_lastc + w]] + pool_recv[w].astype(F32)
        pooled[pl.ds(w * bs, bs), :] = (0.25 * summed).astype(BF16)
    pre = mm(pooled[...], w_c[...])
    sig = jax.nn.sigmoid(pre)
    coarse[...] = (pre * sig).astype(BF16).reshape(win, bs, width)
    c_slope[...] = slope(pre, sig)

    def up_body(q, carry):
        parts = []
        for k in range(quad):
            r = q * quad + k
            parts.append(mm(hot[r], coarse[meta[o_cidx + r]]).astype(BF16))
        block = jnp.concatenate(parts, axis=0)
        up[pl.ds(q * quad, quad)] = block.reshape(quad, bs, width)
        total[pl.ds(q * quad, quad)] += mm(block, w_u[...]).reshape(quad, bs, width)
        return carry

    lax.fori_loop(0, rb // quad, up_body, 0)
    get_cot.wait()
    for copy in halo:
        copy.wait()

    def fine_body(q, carry):
        parts = []
        for k in range(quad):
            r = q * quad + k
            lhs = jnp.concatenate([adj[r, e] for e in range(slots)], axis=1)
            rhs = jnp.concatenate([near[meta[r * slots + e]] for e in range(slots)], axis=0)
            parts.append(mm(lhs, rhs).astype(BF16))
        rows = pl.ds(q * quad, quad)
        flat = (quad * bs, width)
        message = jnp.concatenate(parts, axis=0)
        msg[rows] = message.reshape(quad, bs, width)
        pre = total[rows].reshape(flat) + mm(message, w_m[...])
        sig = jax.nn.sigmoid(pre)
        x = near[pl.ds(half + q * quad, quad)].reshape(flat).astype(F32)
        out_buf[rows] = (x + pre * sig).astype(BF16).reshape(quad, bs, width)
        c = cot[rows].reshape(flat).astype(F32)
        g = (c * slope(pre, sig)).astype(BF16)
        grad[rows] = g.reshape(quad, bs, width)
        back_m[rows] = mm_nt(g, w_m[...]).astype(BF16).reshape(quad, bs, width)
        total[rows] = (c + mm_nt(g, w_s[...])).reshape(quad, bs, width)
        back_u = mm_nt(g, w_u[...]).astype(BF16)
        for k in range(quad):
            r = q * quad + k
            part = mm(hot_t[r], back_u[k * bs : (k + 1) * bs])
            pool_chain[r] = part + pool_chain[meta[o_prevc + r]]
        return carry

    lax.fori_loop(0, rb // quad, fine_body, 0)
    put_out = pltpu.make_async_copy(out_buf, layer_out, out_sem.at[0])
    put_out.start()
    for w in range(win):
        back_send[w] = pool_chain[meta[o_lastc + w]].astype(BF16)
    back_ex = [
        remote(back_send.at[pl.ds(0, cb)], back_recv.at[pl.ds(cb, cb)], 4, left),
        remote(back_send.at[pl.ds(cb, cb)], back_recv.at[pl.ds(0, cb)], 5, right),
    ]
    for copy in back_ex:
        copy.start()

    scale = 1.0 / math.sqrt(n * rb * bs)
    acc[...] = jnp.zeros_like(acc)

    def grads_body(q, carry):
        rows = pl.ds(q * quad, quad)
        flat = (quad * bs, width)
        g = grad[rows].reshape(flat)
        x = near[pl.ds(half + q * quad, quad)].reshape(flat)
        acc[pl.ds(0, width)] += mm_tn(msg[rows].reshape(flat), g)
        acc[pl.ds(width, width)] += mm_tn(up[rows].reshape(flat), g)
        acc[pl.ds(2 * width, width)] += mm_tn(x, g)
        return carry

    lax.fori_loop(0, rb // quad, grads_body, 0)

    def coarse_body(w, carry):
        rows = pl.ds(pl.multiple_of(w * bs, bs), bs)
        part = (pool_chain[meta[o_lastc + w]] * c_slope[rows, :]).astype(BF16)
        acc[pl.ds(3 * width, width)] += mm_tn(pooled[rows, :], part)
        return carry

    lax.fori_loop(0, win, coarse_body, 0)
    acc[...] = acc[...] * scale

    height = acc.shape[0]
    plan = []
    base, seg, index, slot_row = 0, height, 0, 0
    for stride, radix in stages:
        digit = lax.rem(me // stride, radix)
        sub = seg // radix
        plan.append((stride, radix, digit, base, seg, sub, index, slot_row))
        base = base + digit * sub
        seg = sub
        slot_row += (radix - 1) * sub
        index += radix - 1

    def rows_at(start, count):
        return pl.ds(pl.multiple_of(start, 16), count)

    def scatter_start(k):
        stride, radix, digit, base, seg, sub, index, slot_row = plan[k]
        ring_send[k, rows_at(base, seg), :] = acc[rows_at(base, seg), :].astype(BF16)
        copies = []
        for off in range(1, radix):
            other = lax.rem(digit + off, radix)
            copies.append(
                pltpu.make_async_remote_copy(
                    src_ref=ring_send.at[k, rows_at(base + other * sub, sub), :],
                    dst_ref=ring_recv.at[pl.ds(slot_row + (off - 1) * sub, sub), :],
                    send_sem=rs_send.at[index + off - 1],
                    recv_sem=rs_recv.at[index + off - 1],
                    device_id={"blk": me + (other - digit) * stride},
                    device_id_type=MESH,
                )
            )
        for copy in copies:
            copy.start()
        return copies

    def scatter_end(k, copies):
        stride, radix, digit, base, seg, sub, index, slot_row = plan[k]
        for copy in copies:
            copy.wait()
        mine = rows_at(base + digit * sub, sub)
        value = acc[mine, :]
        for off in range(1, radix):
            value = value + ring_recv[pl.ds(slot_row + (off - 1) * sub, sub), :].astype(F32)
        acc[mine, :] = value

    def gather_start(k):
        stride, radix, digit, base, seg, sub, index, slot_row = plan[k]
        mine = rows_at(base + digit * sub, sub)
        copies = []
        for off in range(1, radix):
            other = lax.rem(digit + off, radix)
            copies.append(
                pltpu.make_async_remote_copy(
                    src_ref=gathered.at[mine, :],
                    dst_ref=gathered.at[mine, :],
                    send_sem=ag_send.at[index + off - 1],
                    recv_sem=ag_recv.at[index + off - 1],
                    device_id={"blk": me + (other - digit) * stride},
                    device_id_type=MESH,
                )
            )
        for copy in copies:
            copy.start()
        return copies

    flying = scatter_start(0)

    def flow_body(r, carry):
        prod = mm(adj_t[r], back_m[r])
        for e in range(slots):
            s = r * slots + e
            chain[s] = prod[e * bs : (e + 1) * bs] + chain[meta[o_prev + s]]
        return carry

    lax.fori_loop(0, rb // 2, flow_body, 0)
    scatter_end(0, flying)
    if len(stages) > 1:
        flying = scatter_start(1)
    lax.fori_loop(rb // 2, rb, flow_body, 0)
    for b in range(half):
        row_send[b] = chain[meta[o_last + b]].astype(BF16)
        row_send[half + b] = chain[meta[o_last + half + rb + b]].astype(BF16)
    row_ex = [
        remote(row_send.at[pl.ds(0, half)], row_recv.at[pl.ds(half, half)], 6, left),
        remote(row_send.at[pl.ds(half, half)], row_recv.at[pl.ds(0, half)], 7, right),
    ]
    for copy in row_ex:
        copy.start()
    if len(stages) > 1:
        scatter_end(1, flying)
    if len(stages) > 2:
        flying = scatter_start(2)

    for copy in back_ex:
        copy.wait()
    for w in range(win):
        rows = pl.ds(w * bs, bs)
        summed = pool_chain[meta[o_lastc + w]] + back_recv[w].astype(F32)
        g = (summed * c_slope[rows, :]).astype(BF16)
        back_pooled[w] = mm_nt(g, w_c[...]).astype(BF16)

    def spread_body(r, carry):
        spread = mm(hot[r], back_pooled[meta[o_cidx + r]])
        total[r] += 0.25 * spread + chain[meta[o_last + half + r]]
        return carry

    lax.fori_loop(0, rb, spread_body, 0, unroll=2)

    if len(stages) > 2:
        scatter_end(2, flying)
    for k in range(3, len(stages)):
        scatter_end(k, scatter_start(k))
    stride, radix, digit, base, seg, sub, index, slot_row = plan[-1]
    mine = rows_at(base + digit * sub, sub)
    gathered[mine, :] = acc[mine, :].astype(BF16)
    for k in reversed(range(2, len(stages))):
        for copy in gather_start(k):
            copy.wait()
    flying = gather_start(1) if len(stages) > 1 else []

    put_out.wait()
    for copy in row_ex:
        copy.wait()

    def last_body(r, carry):
        out_buf[r] = (total[r] + row_recv[r].astype(F32)).astype(BF16)
        return carry

    lax.fori_loop(0, rb, last_body, 0, unroll=2)
    put_grad = pltpu.make_async_copy(out_buf, feature_grad, out_sem.at[1])
    put_grad.start()
    for copy in flying:
        copy.wait()
    for copy in gather_start(0):
        copy.wait()
    put_grad.wait()


def on_device(
    features,
    cotangent,
    adjacency,
    block_cols,
    block_count,
    cluster_block,
    cluster_slot,
    w_message,
    w_upward,
    w_self,
    w_coarse,
):
    rb, slots = block_cols.shape
    bs = adjacency.shape[2]
    width = features.shape[1]
    n = lax.axis_size("blk")
    cb = rb // 4
    win = 2 * cb
    count = rb * slots

    smem = pl.BlockSpec(memory_space=pltpu.SMEM)
    meta = pl.pallas_call(
        functools.partial(order_kernel, (n, rb, slots, cb)),
        out_shape=jax.ShapeDtypeStruct((2 * count + 4 * rb + win,), jnp.int32),
        in_specs=[smem] * 3,
        out_specs=smem,
    )(block_cols, block_count, cluster_block)

    stages = stages_of(n)
    links = max(sum(radix - 1 for _, radix in stages), 1)
    height = 4 * width
    rows, seg = 0, height
    for _, radix in stages:
        seg //= radix
        rows += (radix - 1) * seg
    vmem = pl.BlockSpec(memory_space=pltpu.VMEM)
    hbm = pl.BlockSpec(memory_space=pl.ANY)
    blocks = (rb, bs, width)
    outs = pl.pallas_call(
        functools.partial(kernel, (n, rb, slots, bs, cb)),
        out_shape=[
            jax.ShapeDtypeStruct(blocks, BF16),
            jax.ShapeDtypeStruct(blocks, BF16),
        ]
        + [jax.ShapeDtypeStruct((height, width), BF16)],
        in_specs=[smem] + [vmem] * 5 + [hbm] * 3,
        out_specs=[hbm, hbm, vmem],
        scratch_shapes=[
            pltpu.VMEM((2 * rb + 1, bs, width), BF16),
            pltpu.VMEM((rb, slots, bs, bs), BF16),
            pltpu.VMEM((rb, slots * bs, bs), BF16),
            pltpu.VMEM(blocks, BF16),
            pltpu.VMEM(blocks, F32),
            pltpu.VMEM(blocks, BF16),
            pltpu.VMEM(blocks, BF16),
            pltpu.VMEM(blocks, BF16),
            pltpu.VMEM(blocks, BF16),
            pltpu.VMEM((rb, bs, bs), BF16),
            pltpu.VMEM((rb, bs, bs), BF16),
            pltpu.VMEM((count + 1, bs, width), F32),
            pltpu.VMEM((rb + 1, bs, width), F32),
            pltpu.VMEM((win, bs, width), BF16),
            pltpu.VMEM((win, bs, width), BF16),
            pltpu.VMEM((win * bs, width), BF16),
            pltpu.VMEM((win, bs, width), BF16),
            pltpu.VMEM((win * bs, width), F32),
            pltpu.VMEM((win, bs, width), BF16),
            pltpu.VMEM((win, bs, width), BF16),
            pltpu.VMEM((win, bs, width), BF16),
            pltpu.VMEM(blocks, BF16),
            pltpu.VMEM(blocks, BF16),
            pltpu.VMEM(blocks, BF16),
            pltpu.VMEM((height, width), F32),
            pltpu.VMEM((max(len(stages), 1), height, width), BF16),
            pltpu.VMEM((max(rows, 16), width), BF16),
            pltpu.SemaphoreType.DMA((3,)),
            pltpu.SemaphoreType.DMA((2,)),
            pltpu.SemaphoreType.DMA((8,)),
            pltpu.SemaphoreType.DMA((8,)),
            pltpu.SemaphoreType.DMA((links,)),
            pltpu.SemaphoreType.DMA((links,)),
            pltpu.SemaphoreType.DMA((links,)),
            pltpu.SemaphoreType.DMA((links,)),
        ],
        compiler_params=pltpu.CompilerParams(
            collective_id=0, has_side_effects=True, vmem_limit_bytes=56 * 1024 * 1024
        ),
    )(
        meta,
        cluster_slot,
        w_message,
        w_upward,
        w_self,
        w_coarse,
        features.reshape(blocks),
        cotangent.reshape(blocks),
        adjacency,
    )
    pieces = 4 if rb % 4 == 0 else 1
    outs = pl.pallas_call(
        functools.partial(finish_kernel, pieces),
        out_shape=[
            jax.ShapeDtypeStruct(blocks, BF16),
            jax.ShapeDtypeStruct(blocks, BF16),
        ]
        + [jax.ShapeDtypeStruct((width, width), F32)] * 4,
        in_specs=[hbm] * 3,
        out_specs=[hbm, hbm] + [vmem] * 4,
        scratch_shapes=[
            pltpu.VMEM((height, width), BF16),
            pltpu.SemaphoreType.DMA((2 * pieces + 1,)),
        ],
    )(*outs)
    return (outs[0].reshape(features.shape), outs[1].reshape(features.shape), *outs[2:])


def solution(mesh):
    in_specs = (
        P(("group", "blk"), None),
        P(("group", "blk"), None),
        P("blk", None, None, None),
        P("blk", None),
        P("blk"),
        P("blk"),
        P("blk", None),
        P(),
        P(),
        P(),
        P(),
    )
    out_specs = (
        P(("group", "blk"), None),
        P(("group", "blk"), None),
        P("group", None),
        P("group", None),
        P("group", None),
        P("group", None),
    )
    return jax.shard_map(
        on_device, mesh=mesh, in_specs=in_specs, out_specs=out_specs, check_vma=False
    )
```

```python
import functools
import math

import jax
import jax.numpy as jnp
from jax import lax
from jax.experimental import pallas as pl
from jax.experimental.pallas import tpu as pltpu
from jax.sharding import PartitionSpec as P

MESH = pl.DeviceIdType.MESH
BF16 = jnp.bfloat16
F32 = jnp.float32


def mm(left, right):
    return lax.dot_general(left, right, (((1,), (0,)), ((), ())), preferred_element_type=F32)


def mm_nt(left, right):
    return lax.dot_general(left, right, (((1,), (1,)), ((), ())), preferred_element_type=F32)


def mm_tn(left, right):
    return lax.dot_general(left, right, (((0,), (0,)), ((), ())), preferred_element_type=F32)


def slope(value, sigma):
    return sigma * (1.0 + value * (1.0 - sigma))


def stages_of(count):
    stages, stride, rest = [], 1, count
    if rest % 2 == 0:
        stages.append((stride, 2))
        stride, rest = stride * 2, rest // 2
    while rest > 1:
        bits = rest.bit_length() - 1
        radix = 4 if rest % 4 == 0 and bits % 2 == 0 else 2
        stages.append((stride, radix))
        stride, rest = stride * radix, rest // radix
    return stages[:1] + stages[1:][::-1]


def order_kernel(dims, cols_in, counts, clusters, meta):
    n, rb, slots, cb = dims
    half, edge, win = rb // 2, cb // 2, 2 * cb
    me = lax.axis_index("blk")
    count = rb * slots
    o_prev = count
    o_last = 2 * count
    o_cidx = o_last + 2 * rb
    o_prevc = o_cidx + rb
    o_lastc = o_prevc + rb

    def fill(start, size, value):
        def body(i, carry):
            meta[start + i] = value
            return carry

        lax.fori_loop(0, size, body, 0, unroll=8)

    fill(o_last, 2 * rb, count)
    fill(o_lastc, win, rb)

    def row(r, carry):
        live = counts[r]
        for e in range(slots):
            s = r * slots + e
            there = cols_in[s] - (me * rb - half)
            there = jnp.where(there < 0, there + n * rb, there)
            there = jnp.where(there >= n * rb, there - n * rb, there)
            there = jnp.minimum(jnp.maximum(there, 0), 2 * rb - 1)
            on = e < live
            before = meta[o_last + there]
            meta[s] = jnp.where(on, there, 2 * rb)
            meta[o_prev + s] = jnp.where(on, before, count)
            meta[o_last + there] = jnp.where(on, s, before)
        c = clusters[r] - (me * cb - edge)
        c = jnp.where(c < 0, c + n * cb, c)
        c = jnp.where(c >= n * cb, c - n * cb, c)
        c = jnp.minimum(jnp.maximum(c, 0), win - 1)
        meta[o_cidx + r] = c
        meta[o_prevc + r] = meta[o_lastc + c]
        meta[o_lastc + c] = r
        return carry

    lax.fori_loop(0, rb, row, 0)


def finish_kernel(pieces, a, b, g, a_out, b_out, m_out, u_out, s_out, c_out, a_buf, b_buf, buf, sem):
    loads, stores = [], []
    step = a.shape[0] // pieces
    load = pltpu.make_async_copy(g, buf, sem.at[0, 2 * pieces])
    load.start()
    for k in range(pieces):
        rows = pl.ds(k * step, step)
        for j, (src, mid, dst) in enumerate(((a, a_buf, a_out), (b, b_buf, b_out))):
            at = 2 * k + j
            loads.append(pltpu.make_async_copy(src.at[rows], mid.at[rows], sem.at[0, at]))
            stores.append(pltpu.make_async_copy(mid.at[rows], dst.at[rows], sem.at[1, at]))
            loads[-1].start()
    load.wait()
    width = m_out.shape[0]
    for k, out in enumerate((m_out, u_out, s_out, c_out)):
        out[...] = buf[pl.ds(k * width, width), :].astype(F32)
    for come, go in zip(loads, stores):
        come.wait()
        go.start()
    for go in stores:
        go.wait()


def kernel(
    dims,
    meta,
    slot,
    w_m,
    w_u,
    w_s,
    w_c,
    feats,
    cots,
    adjs,
    layer_out,
    feature_grad,
    gathered,
    near,
    adj,
    adj_t,
    cot,
    total,
    msg,
    up,
    grad,
    back_m,
    hot_t,
    hot,
    chain,
    pool_chain,
    pool_send,
    pool_recv,
    pooled,
    coarse,
    c_slope,
    back_send,
    back_recv,
    back_pooled,
    row_send,
    row_recv,
    out_buf,
    acc,
    ring_send,
    ring_recv,
    local_sem,
    out_sem,
    ex_send,
    ex_recv,
    rs_send,
    rs_recv,
    ag_send,
    ag_recv,
):
    n, rb, slots, bs, cb = dims
    width = near.shape[2]
    half, edge, win = rb // 2, cb // 2, 2 * cb
    me = lax.axis_index("blk")
    left, right = lax.rem(me + n - 1, n), lax.rem(me + 1, n)
    stages = stages_of(n)
    o_prev = rb * slots
    o_last = 2 * rb * slots
    o_cidx = o_last + 2 * rb
    o_prevc = o_cidx + rb
    o_lastc = o_prevc + rb

    get_feats = pltpu.make_async_copy(feats, near.at[pl.ds(half, rb)], local_sem.at[0])
    get_cot = pltpu.make_async_copy(cots, cot, local_sem.at[1])
    get_adj = pltpu.make_async_copy(adjs, adj, local_sem.at[2])
    get_feats.start()
    get_adj.start()
    get_cot.start()

    barrier = pltpu.get_barrier_semaphore()
    friends = [left, right]
    for stride, radix in stages:
        digit = lax.rem(me // stride, radix)
        for off in range(1, radix):
            friends.append(me + (lax.rem(digit + off, radix) - digit) * stride)
    for friend in friends:
        pl.semaphore_signal(barrier, inc=1, device_id={"blk": friend}, device_id_type=MESH)
    near[2 * rb] = jnp.zeros((bs, width), BF16)
    pool_chain[rb] = jnp.zeros((bs, width), F32)
    chain[rb * slots] = jnp.zeros((bs, width), F32)
    get_feats.wait()
    pl.semaphore_wait(barrier, len(friends))

    def remote(src, dst, index, to):
        return pltpu.make_async_remote_copy(
            src_ref=src,
            dst_ref=dst,
            send_sem=ex_send.at[index],
            recv_sem=ex_recv.at[index],
            device_id={"blk": to},
            device_id_type=MESH,
        )

    lead = max(half // 4, 1)
    halo = []
    for k, (start, size) in enumerate(((0, lead), (lead, half - lead))):
        for j, (here, there, to) in enumerate(((half, rb + half, left), (rb, 0, right))):
            src = near.at[pl.ds(here + start, size)]
            dst = near.at[pl.ds(there + start, size)]
            halo.append(remote(src, dst, 2 * k + j, to))
    for copy in halo[:2]:
        copy.start()

    def pool_body(r, carry):
        row = slot[pl.ds(r, 1), :]
        ids = lax.broadcasted_iota(jnp.int32, (bs, bs), 0)
        one = jnp.where(ids == row, 1.0, 0.0).astype(BF16)
        hot_t[r] = one
        pool_chain[r] = mm(one, near[half + r]) + pool_chain[meta[o_prevc + r]]
        return carry

    lax.fori_loop(0, rb, pool_body, 0, unroll=2)
    for w in range(win):
        pool_send[w] = pool_chain[meta[o_lastc + w]].astype(BF16)
    pool_ex = [
        remote(pool_send.at[pl.ds(0, cb)], pool_recv.at[pl.ds(cb, cb)], 4, left),
        remote(pool_send.at[pl.ds(cb, cb)], pool_recv.at[pl.ds(0, cb)], 5, right),
    ]
    for copy in pool_ex:
        copy.start()
    for copy in halo[2:]:
        copy.start()

    quad = 4

    def self_body(q, carry):
        x = near[pl.ds(half + q * quad, quad)].reshape(quad * bs, width)
        total[pl.ds(q * quad, quad)] = mm(x, w_s[...]).reshape(quad, bs, width)
        for k in range(quad):
            hot[q * quad + k] = hot_t[q * quad + k].T
        return carry

    lax.fori_loop(0, rb // quad, self_body, 0)
    get_adj.wait()

    def flip_body(r, carry):
        for e in range(slots):
            adj_t[r, pl.ds(e * bs, bs), :] = adj[r, e].T
        return carry

    lax.fori_loop(0, rb, flip_body, 0)

    for copy in pool_ex:
        copy.wait()
    for w in range(win):
        summed = pool_chain[meta[o_lastc + w]] + pool_recv[w].astype(F32)
        pooled[pl.ds(w * bs, bs), :] = (0.25 * summed).astype(BF16)
    pre = mm(pooled[...], w_c[...])
    sig = jax.nn.sigmoid(pre)
    coarse[...] = (pre * sig).astype(BF16).reshape(win, bs, width)
    c_slope[...] = slope(pre, sig)

    def up_body(q, carry):
        parts = []
        for k in range(quad):
            r = q * quad + k
            parts.append(mm(hot[r], coarse[meta[o_cidx + r]]).astype(BF16))
        block = jnp.concatenate(parts, axis=0)
        up[pl.ds(q * quad, quad)] = block.reshape(quad, bs, width)
        total[pl.ds(q * quad, quad)] += mm(block, w_u[...]).reshape(quad, bs, width)
        return carry

    lax.fori_loop(0, rb // quad, up_body, 0)
    get_cot.wait()
    for copy in halo:
        copy.wait()

    def fine_body(q, carry):
        parts = []
        for k in range(quad):
            r = q * quad + k
            lhs = jnp.concatenate([adj[r, e] for e in range(slots)], axis=1)
            rhs = jnp.concatenate([near[meta[r * slots + e]] for e in range(slots)], axis=0)
            parts.append(mm(lhs, rhs).astype(BF16))
        rows = pl.ds(q * quad, quad)
        flat = (quad * bs, width)
        message = jnp.concatenate(parts, axis=0)
        msg[rows] = message.reshape(quad, bs, width)
        pre = total[rows].reshape(flat) + mm(message, w_m[...])
        sig = jax.nn.sigmoid(pre)
        x = near[pl.ds(half + q * quad, quad)].reshape(flat).astype(F32)
        out_buf[rows] = (x + pre * sig).astype(BF16).reshape(quad, bs, width)
        c = cot[rows].reshape(flat).astype(F32)
        g = (c * slope(pre, sig)).astype(BF16)
        grad[rows] = g.reshape(quad, bs, width)
        back_m[rows] = mm_nt(g, w_m[...]).astype(BF16).reshape(quad, bs, width)
        total[rows] = (c + mm_nt(g, w_s[...])).reshape(quad, bs, width)
        back_u = mm_nt(g, w_u[...]).astype(BF16)
        for k in range(quad):
            r = q * quad + k
            part = mm(hot_t[r], back_u[k * bs : (k + 1) * bs])
            pool_chain[r] = part + pool_chain[meta[o_prevc + r]]
        return carry

    lax.fori_loop(0, rb // quad, fine_body, 0)
    put_out = pltpu.make_async_copy(out_buf, layer_out, out_sem.at[0])
    put_out.start()
    for w in range(win):
        back_send[w] = pool_chain[meta[o_lastc + w]].astype(BF16)
    back_ex = [
        remote(back_send.at[pl.ds(0, cb)], back_recv.at[pl.ds(cb, cb)], 6, left),
        remote(back_send.at[pl.ds(cb, cb)], back_recv.at[pl.ds(0, cb)], 7, right),
    ]
    for copy in back_ex:
        copy.start()

    scale = 1.0 / math.sqrt(n * rb * bs)
    acc[...] = jnp.zeros_like(acc)

    def grads_body(q, carry):
        rows = pl.ds(q * quad, quad)
        flat = (quad * bs, width)
        g = grad[rows].reshape(flat)
        x = near[pl.ds(half + q * quad, quad)].reshape(flat)
        acc[pl.ds(0, width)] += mm_tn(msg[rows].reshape(flat), g)
        acc[pl.ds(width, width)] += mm_tn(up[rows].reshape(flat), g)
        acc[pl.ds(2 * width, width)] += mm_tn(x, g)
        return carry

    lax.fori_loop(0, rb // quad, grads_body, 0)

    def coarse_body(w, carry):
        rows = pl.ds(pl.multiple_of(w * bs, bs), bs)
        part = (pool_chain[meta[o_lastc + w]] * c_slope[rows, :]).astype(BF16)
        acc[pl.ds(3 * width, width)] += mm_tn(pooled[rows, :], part)
        return carry

    lax.fori_loop(0, win, coarse_body, 0)
    acc[...] = acc[...] * scale

    height = acc.shape[0]
    plan = []
    base, seg, index, slot_row = 0, height, 0, 0
    for stride, radix in stages:
        digit = lax.rem(me // stride, radix)
        sub = seg // radix
        plan.append((stride, radix, digit, base, seg, sub, index, slot_row))
        base = base + digit * sub
        seg = sub
        slot_row += (radix - 1) * sub
        index += radix - 1

    def rows_at(start, count):
        return pl.ds(pl.multiple_of(start, 16), count)

    def scatter_start(k):
        stride, radix, digit, base, seg, sub, index, slot_row = plan[k]
        ring_send[k, rows_at(base, seg), :] = acc[rows_at(base, seg), :].astype(BF16)
        copies = []
        for off in range(1, radix):
            other = lax.rem(digit + off, radix)
            copies.append(
                pltpu.make_async_remote_copy(
                    src_ref=ring_send.at[k, rows_at(base + other * sub, sub), :],
                    dst_ref=ring_recv.at[pl.ds(slot_row + (off - 1) * sub, sub), :],
                    send_sem=rs_send.at[index + off - 1],
                    recv_sem=rs_recv.at[index + off - 1],
                    device_id={"blk": me + (other - digit) * stride},
                    device_id_type=MESH,
                )
            )
        for copy in copies:
            copy.start()
        return copies

    def scatter_end(k, copies):
        stride, radix, digit, base, seg, sub, index, slot_row = plan[k]
        for copy in copies:
            copy.wait()
        mine = rows_at(base + digit * sub, sub)
        value = acc[mine, :]
        for off in range(1, radix):
            value = value + ring_recv[pl.ds(slot_row + (off - 1) * sub, sub), :].astype(F32)
        acc[mine, :] = value

    def gather_start(k):
        stride, radix, digit, base, seg, sub, index, slot_row = plan[k]
        mine = rows_at(base + digit * sub, sub)
        copies = []
        for off in range(1, radix):
            other = lax.rem(digit + off, radix)
            copies.append(
                pltpu.make_async_remote_copy(
                    src_ref=gathered.at[mine, :],
                    dst_ref=gathered.at[mine, :],
                    send_sem=ag_send.at[index + off - 1],
                    recv_sem=ag_recv.at[index + off - 1],
                    device_id={"blk": me + (other - digit) * stride},
                    device_id_type=MESH,
                )
            )
        for copy in copies:
            copy.start()
        return copies

    flying = scatter_start(0)

    def flow_body(r, carry):
        prod = mm(adj_t[r], back_m[r])
        for e in range(slots):
            s = r * slots + e
            chain[s] = prod[e * bs : (e + 1) * bs] + chain[meta[o_prev + s]]
        return carry

    lax.fori_loop(0, rb // 2, flow_body, 0)
    scatter_end(0, flying)
    if len(stages) > 1:
        flying = scatter_start(1)
    lax.fori_loop(rb // 2, rb, flow_body, 0)
    for b in range(half):
        row_send[b] = chain[meta[o_last + b]].astype(BF16)
        row_send[half + b] = chain[meta[o_last + half + rb + b]].astype(BF16)
    row_ex = []
    piece = half // 4
    for k in range(4):
        for j, (here, there, to) in enumerate(((0, half, left), (half, 0, right))):
            src = row_send.at[pl.ds(here + k * piece, piece)]
            dst = row_recv.at[pl.ds(there + k * piece, piece)]
            row_ex.append(remote(src, dst, 8 + 2 * k + j, to))

    def send_rows(k):
        for copy in row_ex[2 * k : 2 * k + 2]:
            copy.start()

    send_rows(0)
    if len(stages) > 1:
        scatter_end(1, flying)
    if len(stages) > 2:
        flying = scatter_start(2)
    send_rows(1)

    for copy in back_ex:
        copy.wait()
    for w in range(win):
        rows = pl.ds(w * bs, bs)
        summed = pool_chain[meta[o_lastc + w]] + back_recv[w].astype(F32)
        g = (summed * c_slope[rows, :]).astype(BF16)
        back_pooled[w] = mm_nt(g, w_c[...]).astype(BF16)

    def spread_body(r, carry):
        spread = mm(hot[r], back_pooled[meta[o_cidx + r]])
        total[r] += 0.25 * spread + chain[meta[o_last + half + r]]
        return carry

    lax.fori_loop(0, rb, spread_body, 0, unroll=2)

    if len(stages) > 2:
        scatter_end(2, flying)
    for k in range(3, len(stages)):
        scatter_end(k, scatter_start(k))
    stride, radix, digit, base, seg, sub, index, slot_row = plan[-1]
    mine = rows_at(base + digit * sub, sub)
    gathered[mine, :] = acc[mine, :].astype(BF16)
    for k in reversed(range(2, len(stages))):
        copies = gather_start(k)
        if k == 2:
            send_rows(2)
        for copy in copies:
            copy.wait()
    if len(stages) < 3:
        send_rows(2)
    flying = gather_start(1) if len(stages) > 1 else []
    send_rows(3)

    put_out.wait()
    for copy in row_ex:
        copy.wait()

    def last_body(r, carry):
        out_buf[r] = (total[r] + row_recv[r].astype(F32)).astype(BF16)
        return carry

    lax.fori_loop(0, rb, last_body, 0, unroll=2)
    put_grad = pltpu.make_async_copy(out_buf, feature_grad, out_sem.at[1])
    put_grad.start()
    for copy in flying:
        copy.wait()
    for copy in gather_start(0):
        copy.wait()
    put_grad.wait()


def on_device(
    features,
    cotangent,
    adjacency,
    block_cols,
    block_count,
    cluster_block,
    cluster_slot,
    w_message,
    w_upward,
    w_self,
    w_coarse,
):
    rb, slots = block_cols.shape
    bs = adjacency.shape[2]
    width = features.shape[1]
    n = lax.axis_size("blk")
    cb = rb // 4
    win = 2 * cb
    count = rb * slots

    smem = pl.BlockSpec(memory_space=pltpu.SMEM)
    meta = pl.pallas_call(
        functools.partial(order_kernel, (n, rb, slots, cb)),
        out_shape=jax.ShapeDtypeStruct((2 * count + 4 * rb + win,), jnp.int32),
        in_specs=[smem] * 3,
        out_specs=smem,
    )(block_cols.reshape(count), block_count, cluster_block)

    stages = stages_of(n)
    links = max(sum(radix - 1 for _, radix in stages), 1)
    height = 4 * width
    rows, seg = 0, height
    for _, radix in stages:
        seg //= radix
        rows += (radix - 1) * seg
    vmem = pl.BlockSpec(memory_space=pltpu.VMEM)
    hbm = pl.BlockSpec(memory_space=pl.ANY)
    blocks = (rb, bs, width)
    outs = pl.pallas_call(
        functools.partial(kernel, (n, rb, slots, bs, cb)),
        out_shape=[
            jax.ShapeDtypeStruct(blocks, BF16),
            jax.ShapeDtypeStruct(blocks, BF16),
        ]
        + [jax.ShapeDtypeStruct((height, width), BF16)],
        in_specs=[smem] + [vmem] * 5 + [hbm] * 3,
        out_specs=[hbm, hbm, vmem],
        scratch_shapes=[
            pltpu.VMEM((2 * rb + 1, bs, width), BF16),
            pltpu.VMEM((rb, slots, bs, bs), BF16),
            pltpu.VMEM((rb, slots * bs, bs), BF16),
            pltpu.VMEM(blocks, BF16),
            pltpu.VMEM(blocks, F32),
            pltpu.VMEM(blocks, BF16),
            pltpu.VMEM(blocks, BF16),
            pltpu.VMEM(blocks, BF16),
            pltpu.VMEM(blocks, BF16),
            pltpu.VMEM((rb, bs, bs), BF16),
            pltpu.VMEM((rb, bs, bs), BF16),
            pltpu.VMEM((count + 1, bs, width), F32),
            pltpu.VMEM((rb + 1, bs, width), F32),
            pltpu.VMEM((win, bs, width), BF16),
            pltpu.VMEM((win, bs, width), BF16),
            pltpu.VMEM((win * bs, width), BF16),
            pltpu.VMEM((win, bs, width), BF16),
            pltpu.VMEM((win * bs, width), F32),
            pltpu.VMEM((win, bs, width), BF16),
            pltpu.VMEM((win, bs, width), BF16),
            pltpu.VMEM((win, bs, width), BF16),
            pltpu.VMEM(blocks, BF16),
            pltpu.VMEM(blocks, BF16),
            pltpu.VMEM(blocks, BF16),
            pltpu.VMEM((height, width), F32),
            pltpu.VMEM((max(len(stages), 1), height, width), BF16),
            pltpu.VMEM((max(rows, 16), width), BF16),
            pltpu.SemaphoreType.DMA((3,)),
            pltpu.SemaphoreType.DMA((2,)),
            pltpu.SemaphoreType.DMA((16,)),
            pltpu.SemaphoreType.DMA((16,)),
            pltpu.SemaphoreType.DMA((links,)),
            pltpu.SemaphoreType.DMA((links,)),
            pltpu.SemaphoreType.DMA((links,)),
            pltpu.SemaphoreType.DMA((links,)),
        ],
        compiler_params=pltpu.CompilerParams(
            collective_id=0, has_side_effects=True, vmem_limit_bytes=56 * 1024 * 1024
        ),
    )(
        meta,
        cluster_slot,
        w_message,
        w_upward,
        w_self,
        w_coarse,
        features.reshape(blocks),
        cotangent.reshape(blocks),
        adjacency,
    )
    pieces = 4 if rb % 4 == 0 else 1
    outs = pl.pallas_call(
        functools.partial(finish_kernel, pieces),
        out_shape=[
            jax.ShapeDtypeStruct(blocks, BF16),
            jax.ShapeDtypeStruct(blocks, BF16),
        ]
        + [jax.ShapeDtypeStruct((width, width), F32)] * 4,
        in_specs=[hbm] * 3,
        out_specs=[hbm, hbm] + [vmem] * 4,
        scratch_shapes=[
            pltpu.VMEM(blocks, BF16),
            pltpu.VMEM(blocks, BF16),
            pltpu.VMEM((height, width), BF16),
            pltpu.SemaphoreType.DMA((2, 2 * pieces + 1)),
        ],
    )(*outs)
    return (outs[0].reshape(features.shape), outs[1].reshape(features.shape), *outs[2:])


def solution(mesh):
    in_specs = (
        P(("group", "blk"), None),
        P(("group", "blk"), None),
        P("blk", None, None, None),
        P("blk", None),
        P("blk"),
        P("blk"),
        P("blk", None),
        P(),
        P(),
        P(),
        P(),
    )
    out_specs = (
        P(("group", "blk"), None),
        P(("group", "blk"), None),
        P("group", None),
        P("group", None),
        P("group", None),
        P("group", None),
    )
    return jax.shard_map(
        on_device, mesh=mesh, in_specs=in_specs, out_specs=out_specs, check_vma=False
    )
```

```python
import functools
import math

import jax
import jax.numpy as jnp
from jax import lax
from jax.experimental import pallas as pl
from jax.experimental.pallas import tpu as pltpu
from jax.sharding import PartitionSpec as P

MESH = pl.DeviceIdType.MESH
BF16 = jnp.bfloat16
F32 = jnp.float32


def mm(left, right):
    return lax.dot_general(left, right, (((1,), (0,)), ((), ())), preferred_element_type=F32)


def mm_nt(left, right):
    return lax.dot_general(left, right, (((1,), (1,)), ((), ())), preferred_element_type=F32)


def mm_tn(left, right):
    return lax.dot_general(left, right, (((0,), (0,)), ((), ())), preferred_element_type=F32)


def slope(value, sigma):
    return sigma * (1.0 + value * (1.0 - sigma))


def stages_of(count):
    stages, stride, rest = [], 1, count
    if rest % 2 == 0:
        stages.append((stride, 2))
        stride, rest = stride * 2, rest // 2
    while rest > 1:
        bits = rest.bit_length() - 1
        radix = 4 if rest % 4 == 0 and bits % 2 == 0 else 2
        stages.append((stride, radix))
        stride, rest = stride * radix, rest // radix
    return stages[:1] + stages[1:][::-1]


def order_kernel(dims, cols_in, counts, clusters, meta):
    n, rb, slots, cb = dims
    half, edge, win = rb // 2, cb // 2, 2 * cb
    me = lax.axis_index("blk")
    count = rb * slots
    o_prev = count
    o_last = 2 * count
    o_cidx = o_last + 2 * rb
    o_prevc = o_cidx + rb
    o_lastc = o_prevc + rb

    def fill(start, size, value):
        def body(i, carry):
            meta[start + i] = value
            return carry

        lax.fori_loop(0, size, body, 0, unroll=8)

    fill(o_last, 2 * rb, count)
    fill(o_lastc, win, rb)

    def row(r, carry):
        live = counts[r]
        for e in range(slots):
            s = r * slots + e
            there = cols_in[s] - (me * rb - half)
            there = jnp.where(there < 0, there + n * rb, there)
            there = jnp.where(there >= n * rb, there - n * rb, there)
            there = jnp.minimum(jnp.maximum(there, 0), 2 * rb - 1)
            on = e < live
            before = meta[o_last + there]
            meta[s] = jnp.where(on, there, 2 * rb)
            meta[o_prev + s] = jnp.where(on, before, count)
            meta[o_last + there] = jnp.where(on, s, before)
        c = clusters[r] - (me * cb - edge)
        c = jnp.where(c < 0, c + n * cb, c)
        c = jnp.where(c >= n * cb, c - n * cb, c)
        c = jnp.minimum(jnp.maximum(c, 0), win - 1)
        meta[o_cidx + r] = c
        meta[o_prevc + r] = meta[o_lastc + c]
        meta[o_lastc + c] = r
        return carry

    lax.fori_loop(0, rb, row, 0)


def finish_kernel(pieces, a, b, g, a_out, b_out, m_out, u_out, s_out, c_out, a_buf, b_buf, buf, sem):
    loads, stores = [], []
    step = a.shape[0] // pieces
    load = pltpu.make_async_copy(g, buf, sem.at[0, 2 * pieces])
    load.start()
    for k in range(pieces):
        rows = pl.ds(k * step, step)
        for j, (src, mid, dst) in enumerate(((a, a_buf, a_out), (b, b_buf, b_out))):
            at = 2 * k + j
            loads.append(pltpu.make_async_copy(src.at[rows], mid.at[rows], sem.at[0, at]))
            stores.append(pltpu.make_async_copy(mid.at[rows], dst.at[rows], sem.at[1, at]))
            loads[-1].start()
    load.wait()
    width = m_out.shape[0]
    for k, out in enumerate((m_out, u_out, s_out, c_out)):
        out[...] = buf[pl.ds(k * width, width), :].astype(F32)
    for come, go in zip(loads, stores):
        come.wait()
        go.start()
    for go in stores:
        go.wait()


def kernel(
    dims,
    meta,
    slot,
    w_m,
    w_u,
    w_s,
    w_c,
    feats,
    cots,
    adjs,
    layer_out,
    feature_grad,
    gathered,
    near,
    adj,
    adj_t,
    cot,
    total,
    msg,
    up,
    grad,
    back_m,
    hot_t,
    hot,
    chain,
    pool_chain,
    pool_send,
    pool_recv,
    pooled,
    coarse,
    c_slope,
    back_send,
    back_recv,
    back_pooled,
    row_send,
    row_recv,
    out_buf,
    acc,
    ring_send,
    ring_recv,
    local_sem,
    out_sem,
    ex_send,
    ex_recv,
    rs_send,
    rs_recv,
    ag_send,
    ag_recv,
):
    n, rb, slots, bs, cb = dims
    width = near.shape[2]
    half, edge, win = rb // 2, cb // 2, 2 * cb
    me = lax.axis_index("blk")
    left, right = lax.rem(me + n - 1, n), lax.rem(me + 1, n)
    stages = stages_of(n)
    o_prev = rb * slots
    o_last = 2 * rb * slots
    o_cidx = o_last + 2 * rb
    o_prevc = o_cidx + rb
    o_lastc = o_prevc + rb

    get_feats = pltpu.make_async_copy(feats, near.at[pl.ds(half, rb)], local_sem.at[0])
    get_cot = pltpu.make_async_copy(cots, cot, local_sem.at[1])
    get_adj = pltpu.make_async_copy(adjs, adj, local_sem.at[2])
    get_feats.start()
    get_adj.start()
    get_cot.start()

    barrier = pltpu.get_barrier_semaphore()
    friends = [left, right]
    for stride, radix in stages:
        digit = lax.rem(me // stride, radix)
        for off in range(1, radix):
            friends.append(me + (lax.rem(digit + off, radix) - digit) * stride)
    for friend in friends:
        pl.semaphore_signal(barrier, inc=1, device_id={"blk": friend}, device_id_type=MESH)
    near[2 * rb] = jnp.zeros((bs, width), BF16)
    pool_chain[rb] = jnp.zeros((bs, width), F32)
    chain[rb * slots] = jnp.zeros((bs, width), F32)
    get_feats.wait()
    pl.semaphore_wait(barrier, len(friends))

    def remote(src, dst, index, to):
        return pltpu.make_async_remote_copy(
            src_ref=src,
            dst_ref=dst,
            send_sem=ex_send.at[index],
            recv_sem=ex_recv.at[index],
            device_id={"blk": to},
            device_id_type=MESH,
        )

    lead = max(half // 4, 1)
    halo = []
    for k, (start, size) in enumerate(((0, lead), (lead, half - lead))):
        for j, (here, there, to) in enumerate(((half, rb + half, left), (rb, 0, right))):
            src = near.at[pl.ds(here + start, size)]
            dst = near.at[pl.ds(there + start, size)]
            halo.append(remote(src, dst, 2 * k + j, to))
    for copy in halo[:2]:
        copy.start()

    def pool_body(r, carry):
        row = slot[pl.ds(r, 1), :]
        ids = lax.broadcasted_iota(jnp.int32, (bs, bs), 0)
        one = jnp.where(ids == row, 1.0, 0.0).astype(BF16)
        hot_t[r] = one
        pool_chain[r] = mm(one, near[half + r]) + pool_chain[meta[o_prevc + r]]
        return carry

    lax.fori_loop(0, rb, pool_body, 0, unroll=2)
    for w in range(win):
        pool_send[w] = pool_chain[meta[o_lastc + w]].astype(BF16)
    pool_ex = [
        remote(pool_send.at[pl.ds(0, cb)], pool_recv.at[pl.ds(cb, cb)], 4, left),
        remote(pool_send.at[pl.ds(cb, cb)], pool_recv.at[pl.ds(0, cb)], 5, right),
    ]
    for copy in pool_ex:
        copy.start()
    for copy in halo[2:]:
        copy.start()

    quad = 4

    def self_body(q, carry):
        x = near[pl.ds(half + q * quad, quad)].reshape(quad * bs, width)
        total[pl.ds(q * quad, quad)] = mm(x, w_s[...]).reshape(quad, bs, width)
        for k in range(quad):
            hot[q * quad + k] = hot_t[q * quad + k].T
        return carry

    lax.fori_loop(0, rb // quad, self_body, 0)
    get_adj.wait()

    def flip_body(r, carry):
        for e in range(slots):
            adj_t[r, pl.ds(e * bs, bs), :] = adj[r, e].T
        return carry

    lax.fori_loop(0, rb, flip_body, 0)

    for copy in pool_ex:
        copy.wait()
    for w in range(win):
        summed = pool_chain[meta[o_lastc + w]] + pool_recv[w].astype(F32)
        pooled[pl.ds(w * bs, bs), :] = (0.25 * summed).astype(BF16)
    pre = mm(pooled[...], w_c[...])
    sig = jax.nn.sigmoid(pre)
    coarse[...] = (pre * sig).astype(BF16).reshape(win, bs, width)
    c_slope[...] = slope(pre, sig)

    def up_body(q, carry):
        parts = []
        for k in range(quad):
            r = q * quad + k
            parts.append(mm(hot[r], coarse[meta[o_cidx + r]]).astype(BF16))
        block = jnp.concatenate(parts, axis=0)
        up[pl.ds(q * quad, quad)] = block.reshape(quad, bs, width)
        total[pl.ds(q * quad, quad)] += mm(block, w_u[...]).reshape(quad, bs, width)
        return carry

    lax.fori_loop(0, rb // quad, up_body, 0)
    get_cot.wait()
    for copy in halo:
        copy.wait()

    def fine_body(q, carry):
        parts = []
        for k in range(quad):
            r = q * quad + k
            lhs = jnp.concatenate([adj[r, e] for e in range(slots)], axis=1)
            rhs = jnp.concatenate([near[meta[r * slots + e]] for e in range(slots)], axis=0)
            parts.append(mm(lhs, rhs).astype(BF16))
        rows = pl.ds(q * quad, quad)
        flat = (quad * bs, width)
        message = jnp.concatenate(parts, axis=0)
        msg[rows] = message.reshape(quad, bs, width)
        pre = total[rows].reshape(flat) + mm(message, w_m[...])
        sig = jax.nn.sigmoid(pre)
        x = near[pl.ds(half + q * quad, quad)].reshape(flat).astype(F32)
        out_buf[rows] = (x + pre * sig).astype(BF16).reshape(quad, bs, width)
        c = cot[rows].reshape(flat).astype(F32)
        g = (c * slope(pre, sig)).astype(BF16)
        grad[rows] = g.reshape(quad, bs, width)
        back_m[rows] = mm_nt(g, w_m[...]).astype(BF16).reshape(quad, bs, width)
        total[rows] = (c + mm_nt(g, w_s[...])).reshape(quad, bs, width)
        back_u = mm_nt(g, w_u[...]).astype(BF16)
        for k in range(quad):
            r = q * quad + k
            part = mm(hot_t[r], back_u[k * bs : (k + 1) * bs])
            pool_chain[r] = part + pool_chain[meta[o_prevc + r]]
        return carry

    lax.fori_loop(0, rb // quad, fine_body, 0)
    put_out = pltpu.make_async_copy(out_buf, layer_out, out_sem.at[0])
    put_out.start()
    for w in range(win):
        back_send[w] = pool_chain[meta[o_lastc + w]].astype(BF16)
    back_ex = [
        remote(back_send.at[pl.ds(0, cb)], back_recv.at[pl.ds(cb, cb)], 6, left),
        remote(back_send.at[pl.ds(cb, cb)], back_recv.at[pl.ds(0, cb)], 7, right),
    ]

    scale = 1.0 / math.sqrt(n * rb * bs)
    acc[...] = jnp.zeros_like(acc)

    def grads_body(q, carry):
        rows = pl.ds(q * quad, quad)
        flat = (quad * bs, width)
        g = grad[rows].reshape(flat)
        x = near[pl.ds(half + q * quad, quad)].reshape(flat)
        acc[pl.ds(0, width)] += mm_tn(msg[rows].reshape(flat), g)
        acc[pl.ds(width, width)] += mm_tn(up[rows].reshape(flat), g)
        acc[pl.ds(2 * width, width)] += mm_tn(x, g)
        return carry

    lax.fori_loop(0, rb // quad, grads_body, 0)

    def coarse_body(w, carry):
        rows = pl.ds(pl.multiple_of(w * bs, bs), bs)
        part = (pool_chain[meta[o_lastc + w]] * c_slope[rows, :]).astype(BF16)
        acc[pl.ds(3 * width, width)] += mm_tn(pooled[rows, :], part)
        return carry

    lax.fori_loop(0, win, coarse_body, 0)
    acc[...] = acc[...] * scale

    height = acc.shape[0]
    plan = []
    base, seg, index, slot_row = 0, height, 0, 0
    for stride, radix in stages:
        digit = lax.rem(me // stride, radix)
        sub = seg // radix
        plan.append((stride, radix, digit, base, seg, sub, index, slot_row))
        base = base + digit * sub
        seg = sub
        slot_row += (radix - 1) * sub
        index += radix - 1

    def rows_at(start, count):
        return pl.ds(pl.multiple_of(start, 16), count)

    def scatter_start(k):
        stride, radix, digit, base, seg, sub, index, slot_row = plan[k]
        ring_send[k, rows_at(base, seg), :] = acc[rows_at(base, seg), :].astype(BF16)
        copies = []
        for off in range(1, radix):
            other = lax.rem(digit + off, radix)
            copies.append(
                pltpu.make_async_remote_copy(
                    src_ref=ring_send.at[k, rows_at(base + other * sub, sub), :],
                    dst_ref=ring_recv.at[pl.ds(slot_row + (off - 1) * sub, sub), :],
                    send_sem=rs_send.at[index + off - 1],
                    recv_sem=rs_recv.at[index + off - 1],
                    device_id={"blk": me + (other - digit) * stride},
                    device_id_type=MESH,
                )
            )
        for copy in copies:
            copy.start()
        return copies

    def scatter_end(k, copies):
        stride, radix, digit, base, seg, sub, index, slot_row = plan[k]
        for copy in copies:
            copy.wait()
        mine = rows_at(base + digit * sub, sub)
        value = acc[mine, :]
        for off in range(1, radix):
            value = value + ring_recv[pl.ds(slot_row + (off - 1) * sub, sub), :].astype(F32)
        acc[mine, :] = value

    def gather_start(k):
        stride, radix, digit, base, seg, sub, index, slot_row = plan[k]
        mine = rows_at(base + digit * sub, sub)
        copies = []
        for off in range(1, radix):
            other = lax.rem(digit + off, radix)
            copies.append(
                pltpu.make_async_remote_copy(
                    src_ref=gathered.at[mine, :],
                    dst_ref=gathered.at[mine, :],
                    send_sem=ag_send.at[index + off - 1],
                    recv_sem=ag_recv.at[index + off - 1],
                    device_id={"blk": me + (other - digit) * stride},
                    device_id_type=MESH,
                )
            )
        for copy in copies:
            copy.start()
        return copies

    flying = scatter_start(0)
    for copy in back_ex:
        copy.start()

    def flow_body(r, carry):
        prod = mm(adj_t[r], back_m[r])
        for e in range(slots):
            s = r * slots + e
            chain[s] = prod[e * bs : (e + 1) * bs] + chain[meta[o_prev + s]]
        return carry

    lax.fori_loop(0, rb // 2, flow_body, 0)
    scatter_end(0, flying)
    if len(stages) > 1:
        flying = scatter_start(1)
    lax.fori_loop(rb // 2, rb, flow_body, 0)
    for b in range(half):
        row_send[b] = chain[meta[o_last + b]].astype(BF16)
        row_send[half + b] = chain[meta[o_last + half + rb + b]].astype(BF16)
    row_ex = []
    piece = half // 4
    for k in range(4):
        for j, (here, there, to) in enumerate(((0, half, left), (half, 0, right))):
            src = row_send.at[pl.ds(here + k * piece, piece)]
            dst = row_recv.at[pl.ds(there + k * piece, piece)]
            row_ex.append(remote(src, dst, 8 + 2 * k + j, to))

    def send_rows(k):
        for copy in row_ex[2 * k : 2 * k + 2]:
            copy.start()

    send_rows(0)
    if len(stages) > 1:
        scatter_end(1, flying)
    if len(stages) > 2:
        flying = scatter_start(2)
    send_rows(1)

    if len(stages) > 2:
        scatter_end(2, flying)
    for k in range(3, len(stages)):
        scatter_end(k, scatter_start(k))
    stride, radix, digit, base, seg, sub, index, slot_row = plan[-1]
    mine = rows_at(base + digit * sub, sub)
    gathered[mine, :] = acc[mine, :].astype(BF16)
    for k in reversed(range(2, len(stages))):
        copies = gather_start(k)
        if k == 2:
            send_rows(2)
        for copy in copies:
            copy.wait()
    if len(stages) < 3:
        send_rows(2)
    flying = gather_start(1) if len(stages) > 1 else []
    send_rows(3)

    for copy in back_ex:
        copy.wait()
    for w in range(win):
        rows = pl.ds(w * bs, bs)
        summed = pool_chain[meta[o_lastc + w]] + back_recv[w].astype(F32)
        g = (summed * c_slope[rows, :]).astype(BF16)
        back_pooled[w] = mm_nt(g, w_c[...]).astype(BF16)

    def spread_body(r, carry):
        spread = mm(hot[r], back_pooled[meta[o_cidx + r]])
        total[r] += 0.25 * spread + chain[meta[o_last + half + r]]
        return carry

    lax.fori_loop(0, rb, spread_body, 0, unroll=2)

    for copy in flying:
        copy.wait()
    flying = gather_start(0)
    put_out.wait()
    for copy in row_ex:
        copy.wait()

    def last_body(r, carry):
        out_buf[r] = (total[r] + row_recv[r].astype(F32)).astype(BF16)
        return carry

    lax.fori_loop(0, rb, last_body, 0, unroll=2)
    put_grad = pltpu.make_async_copy(out_buf, feature_grad, out_sem.at[1])
    put_grad.start()
    for copy in flying:
        copy.wait()
    put_grad.wait()


def on_device(
    features,
    cotangent,
    adjacency,
    block_cols,
    block_count,
    cluster_block,
    cluster_slot,
    w_message,
    w_upward,
    w_self,
    w_coarse,
):
    rb, slots = block_cols.shape
    bs = adjacency.shape[2]
    width = features.shape[1]
    n = lax.axis_size("blk")
    cb = rb // 4
    win = 2 * cb
    count = rb * slots

    smem = pl.BlockSpec(memory_space=pltpu.SMEM)
    meta = pl.pallas_call(
        functools.partial(order_kernel, (n, rb, slots, cb)),
        out_shape=jax.ShapeDtypeStruct((2 * count + 4 * rb + win,), jnp.int32),
        in_specs=[smem] * 3,
        out_specs=smem,
    )(block_cols.reshape(count), block_count, cluster_block)

    stages = stages_of(n)
    links = max(sum(radix - 1 for _, radix in stages), 1)
    height = 4 * width
    rows, seg = 0, height
    for _, radix in stages:
        seg //= radix
        rows += (radix - 1) * seg
    vmem = pl.BlockSpec(memory_space=pltpu.VMEM)
    hbm = pl.BlockSpec(memory_space=pl.ANY)
    blocks = (rb, bs, width)
    outs = pl.pallas_call(
        functools.partial(kernel, (n, rb, slots, bs, cb)),
        out_shape=[
            jax.ShapeDtypeStruct(blocks, BF16),
            jax.ShapeDtypeStruct(blocks, BF16),
        ]
        + [jax.ShapeDtypeStruct((height, width), BF16)],
        in_specs=[smem] + [vmem] * 5 + [hbm] * 3,
        out_specs=[hbm, hbm, vmem],
        scratch_shapes=[
            pltpu.VMEM((2 * rb + 1, bs, width), BF16),
            pltpu.VMEM((rb, slots, bs, bs), BF16),
            pltpu.VMEM((rb, slots * bs, bs), BF16),
            pltpu.VMEM(blocks, BF16),
            pltpu.VMEM(blocks, F32),
            pltpu.VMEM(blocks, BF16),
            pltpu.VMEM(blocks, BF16),
            pltpu.VMEM(blocks, BF16),
            pltpu.VMEM(blocks, BF16),
            pltpu.VMEM((rb, bs, bs), BF16),
            pltpu.VMEM((rb, bs, bs), BF16),
            pltpu.VMEM((count + 1, bs, width), F32),
            pltpu.VMEM((rb + 1, bs, width), F32),
            pltpu.VMEM((win, bs, width), BF16),
            pltpu.VMEM((win, bs, width), BF16),
            pltpu.VMEM((win * bs, width), BF16),
            pltpu.VMEM((win, bs, width), BF16),
            pltpu.VMEM((win * bs, width), F32),
            pltpu.VMEM((win, bs, width), BF16),
            pltpu.VMEM((win, bs, width), BF16),
            pltpu.VMEM((win, bs, width), BF16),
            pltpu.VMEM(blocks, BF16),
            pltpu.VMEM(blocks, BF16),
            pltpu.VMEM(blocks, BF16),
            pltpu.VMEM((height, width), F32),
            pltpu.VMEM((max(len(stages), 1), height, width), BF16),
            pltpu.VMEM((max(rows, 16), width), BF16),
            pltpu.SemaphoreType.DMA((3,)),
            pltpu.SemaphoreType.DMA((2,)),
            pltpu.SemaphoreType.DMA((16,)),
            pltpu.SemaphoreType.DMA((16,)),
            pltpu.SemaphoreType.DMA((links,)),
            pltpu.SemaphoreType.DMA((links,)),
            pltpu.SemaphoreType.DMA((links,)),
            pltpu.SemaphoreType.DMA((links,)),
        ],
        compiler_params=pltpu.CompilerParams(
            collective_id=0, has_side_effects=True, vmem_limit_bytes=56 * 1024 * 1024
        ),
    )(
        meta,
        cluster_slot,
        w_message,
        w_upward,
        w_self,
        w_coarse,
        features.reshape(blocks),
        cotangent.reshape(blocks),
        adjacency,
    )
    pieces = 4 if rb % 4 == 0 else 1
    outs = pl.pallas_call(
        functools.partial(finish_kernel, pieces),
        out_shape=[
            jax.ShapeDtypeStruct(blocks, BF16),
            jax.ShapeDtypeStruct(blocks, BF16),
        ]
        + [jax.ShapeDtypeStruct((width, width), F32)] * 4,
        in_specs=[hbm] * 3,
        out_specs=[hbm, hbm] + [vmem] * 4,
        scratch_shapes=[
            pltpu.VMEM(blocks, BF16),
            pltpu.VMEM(blocks, BF16),
            pltpu.VMEM((height, width), BF16),
            pltpu.SemaphoreType.DMA((2, 2 * pieces + 1)),
        ],
    )(*outs)
    return (outs[0].reshape(features.shape), outs[1].reshape(features.shape), *outs[2:])


def solution(mesh):
    in_specs = (
        P(("group", "blk"), None),
        P(("group", "blk"), None),
        P("blk", None, None, None),
        P("blk", None),
        P("blk"),
        P("blk"),
        P("blk", None),
        P(),
        P(),
        P(),
        P(),
    )
    out_specs = (
        P(("group", "blk"), None),
        P(("group", "blk"), None),
        P("group", None),
        P("group", None),
        P("group", None),
        P("group", None),
    )
    return jax.shard_map(
        on_device, mesh=mesh, in_specs=in_specs, out_specs=out_specs, check_vma=False
    )
```
